128 devices in a mesh: frame: 4 (over y_hi, core), slab: 32 (over y_lo, x, z).
Axes of the slice: x: 4, y: 4 (y_hi: 2, y_lo: 2; y = y_hi * 2 + y_lo), z: 4, core: 2. Of those that a mesh axis runs over, the one named last changes fastest.
Arguments:
- template: float32 [256, 32, 256], P('slab'), may hold values from -6 to 6
- displacement: float32 [8, 256, 32, 256], P('frame', 'slab'), may hold values from -8 to 8
- coil_images: bfloat16 [8, 2, 24, 256, 32, 256], P('frame', None, None, 'slab'), may hold values from -6 to 6
- sensitivities: bfloat16 [2, 24, 256, 32, 256], P(None, None, 'slab'), may hold values from -0.875 to 0.875
Outputs:
- refreshed_template: float32 [256, 32, 256], P('slab')
- new_displacement: float32 [8, 256, 32, 256], P('frame', 'slab')
The draws below stay inside these ranges and needn't reach their ends.
All inputs are finite; a program needn't handle non-finite values.
Results may differ from the reference program's by a relative error of at most 0.0003.
Values sent between devices are 32-bit elements; how exact they have to be, the bound alone decides.
A program may use at most 128 MiB of HBM per device.

```python
import jax
import jax.numpy as jnp
from jax import lax

COILS = 24
NY = 256
XW = 32
BOUND = 8
RADIUS = 4
FRAMES = 8
NZ = 256


def level_of(key, shape, pieces, smallest, high):
    gain = 1.0
    for position, blocks in pieces:
        heights = jax.random.uniform(jax.random.fold_in(jax.random.fold_in(key, 6), position), (blocks,), jnp.float32, smallest / len(pieces), high / len(pieces))
        gain = gain * jnp.repeat(jnp.exp(heights), shape[position] // blocks).reshape((-1,) + (1,) * (len(shape) - 1 - position))
    return gain


def scatter_about(stream_key, shape, scale, limit, pieces=(), held_as=jnp.bfloat16):
    result = jax.random.normal(stream_key, shape, jnp.float32) * scale
    if len(pieces) > 0:
        result = level_of(stream_key, shape, pieces, -0.22, 0.18) * result
    return jnp.clip(result, min=-limit, max=limit).astype(held_as)


def setup_inputs(seed: int = 0) -> dict:
    arg_keys = jax.random.split(jax.random.key(seed), 5)
    template = scatter_about(arg_keys[0], (NZ, XW, NY), 1.0, 6.0, ((0, 32),), jnp.float32)
    displacement = jnp.clip(jax.random.uniform(arg_keys[1], (FRAMES, NZ, XW, NY), jnp.float32, -8.0, 8.0) * level_of(arg_keys[1], (FRAMES, NZ, XW, NY), ((0, 4), (1, 32)), -0.4, 0.0), -8.0, 8.0)
    coil_images = scatter_about(arg_keys[2], (FRAMES, 2, COILS, NZ, XW, NY), 1.0, 6.0, ((0, 4), (3, 32)))
    sensitivities = scatter_about(arg_keys[3], (2, COILS, NZ, XW, NY), (2 * COILS) ** -0.5, 0.875, ((2, 32),))
    return dict(template=template, displacement=displacement, coil_images=coil_images, sensitivities=sensitivities)


def tent_weight(values):
    return jnp.maximum(0.0, 1.0 - jnp.abs(values))


def pad_planes(field, width):
    widths = [(0, 0)] * field.ndim
    widths[field.ndim - 3] = (width, width)
    return jnp.pad(field, widths)


def warp_planes(extended, displace, extent):
    planes = displace.shape[-3]
    summed = jnp.zeros(displace.shape, jnp.float32)
    for offset in range(-extent, extent + 1):
        source = extended[..., extent + offset:extent + offset + planes, :, :]
        summed = summed + tent_weight(displace - offset) * source
    return summed


def adjoint_planes(displace_ext, residual_ext, extent):
    planes = displace_ext.shape[-3] - 2 * extent
    summed = jnp.zeros(displace_ext.shape[:-3] + (planes,) + displace_ext.shape[-2:], jnp.float32)
    for offset in range(-extent, extent + 1):
        lower = extent - offset
        moved_from = displace_ext[..., lower:lower + planes, :, :]
        values = residual_ext[..., lower:lower + planes, :, :]
        summed = summed + tent_weight(moved_from - offset) * values
    return summed


def gauss_weights(radius):
    offsets_list = jnp.arange(-radius, radius + 1).astype(jnp.float32)
    spread = radius * 0.5
    unscaled = jnp.exp(-offsets_list * offsets_list / (2.0 * spread * spread))
    return unscaled / jnp.sum(unscaled)


def gauss_table(length, radius):
    indices = jnp.arange(length)
    apart = indices[:, None] - indices[None, :]
    distance = apart.astype(jnp.float32)
    spread = radius * 0.5
    offsets_list = jnp.arange(-radius, radius + 1).astype(jnp.float32)
    normalizer = jnp.sum(jnp.exp(-offsets_list * offsets_list / (2.0 * spread * spread)))
    unscaled = jnp.where(jnp.abs(apart) <= radius, jnp.exp(-distance * distance / (2.0 * spread * spread)), 0.0)
    return unscaled / normalizer


def smooth_field(extended, radius, planes):
    weights = gauss_weights(radius)
    summed = jnp.zeros(extended.shape[:-3] + (planes,) + extended.shape[-2:], jnp.float32)
    for offset in range(-radius, radius + 1):
        summed = summed + weights[offset + radius] * extended[..., radius + offset:radius + offset + planes, :, :]
    table_y = gauss_table(summed.shape[-1], radius)
    table_x = gauss_table(summed.shape[-2], radius)
    along_y = jnp.einsum("...xy,yw->...xw", summed, table_y, precision=lax.Precision.HIGHEST)
    return jnp.einsum("...xy,xv->...vy", along_y, table_x, precision=lax.Precision.HIGHEST)


def demons_step(displace, combined, template_ext, extent):
    planes = displace.shape[-3]
    warped_new = warp_planes(template_ext, displace, extent)
    mismatch = combined - warped_new
    interior = template_ext[extent:extent + planes]
    grad_z = (template_ext[extent + 1:extent + 1 + planes] - template_ext[extent - 1:extent - 1 + planes]) * 0.5
    padded_x = jnp.pad(interior, ((0, 0), (1, 1), (0, 0)))
    grad_x = (padded_x[:, 2:, :] - padded_x[:, :-2, :]) * 0.5
    padded_y = jnp.pad(interior, ((0, 0), (0, 0), (1, 1)))
    grad_y = (padded_y[:, :, 2:] - padded_y[:, :, :-2]) * 0.5
    gradient_sq = grad_x * grad_x + grad_y * grad_y + grad_z * grad_z
    demons_force = mismatch * grad_z / (gradient_sq + mismatch * mismatch + 1.0)
    return displace + demons_force


def reference(template, displacement, coil_images, sensitivities):
    sens_float = sensitivities.astype(jnp.float32)
    energy = jnp.einsum("pczxy,pczxy->zxy", sens_float, sens_float)

    def combine(one_frame):
        return jnp.einsum("pczxy,pczxy->zxy", one_frame.astype(jnp.float32), sens_float)

    combined = lax.map(combine, coil_images)
    warped = warp_planes(pad_planes(template, BOUND), displacement, BOUND)
    residual_back = combined - energy * warped
    adjoint = adjoint_planes(pad_planes(displacement, BOUND), pad_planes(residual_back, BOUND), BOUND)
    refreshed = template + jnp.sum(adjoint, axis=0) / FRAMES
    refreshed_ext = pad_planes(refreshed, BOUND)
    moved = demons_step(displacement, combined, refreshed_ext, BOUND)
    smoothed = smooth_field(pad_planes(moved, RADIUS), RADIUS, moved.shape[1])
    return refreshed, BOUND * jnp.tanh(smoothed / BOUND)
```

```python
import functools

import jax
import jax.numpy as jnp
import numpy as np
from jax import lax
from jax.experimental import pallas as pl
from jax.experimental.pallas import tpu as pltpu
from jax.sharding import PartitionSpec as P

BOUND = 8
RADIUS = 4
ROWS = 8
LANES = 128
CHUNK = 16
GROUPS = 4
MESH = pl.DeviceIdType.MESH
F32 = jnp.float32
BF16 = jnp.bfloat16


def gauss_weights():
    j = np.arange(-RADIUS, RADIUS + 1, dtype=np.float64)
    spread = RADIUS * 0.5
    w = np.exp(-j * j / (2.0 * spread * spread))
    return w / w.sum()


def gauss_table(length):
    w = gauss_weights()
    table = np.zeros((length, length), np.float64)
    for j in range(-RADIUS, RADIUS + 1):
        table += w[j + RADIUS] * np.eye(length, k=j)
    return table


def split_table(table):
    hi = table.astype(np.float32).astype(BF16)
    lo = (table - hi.astype(np.float64)).astype(np.float32).astype(BF16)
    return hi, lo


def locate(d):
    m3 = d >= 0.0
    r = jnp.where(m3, d, d + 8.0)
    m2 = r >= 4.0
    r = jnp.where(m2, r - 4.0, r)
    m1 = r >= 2.0
    r = jnp.where(m1, r - 2.0, r)
    m0 = r >= 1.0
    t = jnp.where(m0, r - 1.0, r)
    return m3, m2, m1, m0, t


def gather_line(place, plane):
    m3, m2, m1, m0, t = place
    a = [plane(j) for j in range(17)]
    b = [jnp.where(m3, a[j + 8], a[j]) for j in range(9)]
    c = [jnp.where(m2, b[j + 4], b[j]) for j in range(5)]
    e = [jnp.where(m1, c[j + 2], c[j]) for j in range(3)]
    lo = jnp.where(m0, e[1], e[0])
    hi = jnp.where(m0, e[2], e[1])
    return lo + t * (hi - lo)


def scatter_line(place, value):
    m3, m2, m1, m0, t = place
    hi = t * value
    lo = value - hi
    zero = jnp.zeros_like(value)
    e = [jnp.where(m0, zero, lo), jnp.where(m0, lo, hi), jnp.where(m0, hi, zero)]

    def spread(src, mask, step):
        n = len(src)
        out = []
        for j in range(n + step):
            low = src[j] if j < n else zero
            high = src[j - step] if j >= step else zero
            out.append(jnp.where(mask, high, low))
        return out

    return spread(spread(spread(e, m1, 2), m2, 4), m3, 8)


def kernel(cfg, tmpl, disp, coil, sens, ty_hi_h, ty_lo_h, kx_hi_h, kx_lo_h, out_t, out_d,
           tx, rx, dv, cb, sb, comb, ener, adj, radj, rlo, rhi, csum, rc, mv, gz, gs,
           shi, slo, obuf, ty_hi, ty_lo, kx_hi, kx_lo, lsem, ssem, rsem):
    n_slab, frames_all, coils = cfg
    nf, planes = dv.shape[0], dv.shape[1]
    wide = dv.shape[2]
    ny = dv.shape[3]
    n_rb = wide // ROWS
    n_chunk = wide // CHUNK
    per = planes // GROUPS
    f = lax.axis_index("frame")
    s = lax.axis_index("slab")
    h = lax.rem(f, 2)
    mate = f + 1 - 2 * h
    across = lax.rem(f + 2, 4)
    above = lax.rem(s + 1, n_slab)
    below = lax.rem(s + n_slab - 1, n_slab)
    has_above = s < n_slab - 1
    has_below = s > 0
    to_mate, to_across = (mate, s), (across, s)
    to_above, to_below = (f, above), (f, below)

    counter = [0]

    def local(src, dst):
        copy = pltpu.make_async_copy(src, dst, lsem.at[counter[0]])
        counter[0] += 1
        copy.start()
        return copy

    load_t = [local(tmpl.at[:, pl.ds(ROWS * b, ROWS), :], tx.at[b, pl.ds(BOUND, planes)]) for b in range(n_rb)]
    load_d = local(disp, dv)
    load_c = {}
    for c in range(n_chunk):
        for g in range(GROUPS):
            zs, xs = pl.ds(per * g, per), pl.ds(CHUNK * c, CHUNK)
            load_c[c, g] = (
                local(sens.at[:, :, zs, xs, :], sb.at[c, g]),
                local(coil.at[:, :, :, zs, xs, :], cb.at[c, g]),
            )
    load_k = [local(a, b) for a, b in ((ty_hi_h, ty_hi), (ty_lo_h, ty_lo), (kx_hi_h, kx_hi), (kx_lo_h, kx_lo))]

    barrier = pltpu.get_barrier_semaphore()
    for dev in (to_mate, to_across, to_above, to_below):
        pl.semaphore_signal(barrier, inc=1, device_id=dev, device_id_type=MESH)
    pl.semaphore_wait(barrier, 4)

    rcount = [0]
    pending = []

    class Remote:
        def __init__(self, src, dst, dev, send_if=None, recv_if=None):
            n = rcount[0]
            rcount[0] += 1
            self.copy = pltpu.make_async_remote_copy(
                src_ref=src, dst_ref=dst, send_sem=ssem.at[n], recv_sem=rsem.at[n],
                device_id=dev, device_id_type=MESH)
            self.send_if, self.recv_if = send_if, recv_if
            if send_if is None:
                self.copy.start()
            else:
                pl.when(send_if)(lambda: self.copy.start())
            pending.append(self)

        def recv(self):
            if self.recv_if is None:
                self.copy.wait_recv()
            else:
                pl.when(self.recv_if)(lambda: self.copy.wait_recv())

        def sent(self):
            if self.send_if is None:
                self.copy.wait_send()
            else:
                pl.when(self.send_if)(lambda: self.copy.wait_send())

    def up(src, dst):
        return Remote(src, dst, to_above, has_above, has_below)

    def down(src, dst):
        return Remote(src, dst, to_below, has_below, has_above)

    own = pl.ds(BOUND, planes)
    low = pl.ds(0, BOUND)
    high = pl.ds(BOUND + planes, BOUND)
    wire = {}

    def zero_edges(clear_low, clear_high):
        @pl.when(s == 0)
        def _():
            for ref, *index in clear_low:
                ref[tuple(index)] = jnp.zeros_like(ref[tuple(index)])

        @pl.when(s == n_slab - 1)
        def _():
            for ref, *index in clear_high:
                ref[tuple(index)] = jnp.zeros_like(ref[tuple(index)])

    def template_out(c):
        rb = 2 * c + h
        wire["tu", c] = up(tx.at[rb, own], tx.at[rb, low])
        wire["td", c] = down(tx.at[rb, own], tx.at[rb, high])

    def template_pass(c):
        rb = 2 * c + h
        wire["tu", c].recv()
        wire["td", c].recv()
        wire["tfl", c] = Remote(tx.at[rb, low], tx.at[rb, low], to_mate, has_below, has_below)
        wire["tfh", c] = Remote(tx.at[rb, high], tx.at[rb, high], to_mate, has_above, has_above)

    def template_in(c):
        wire["tfl", c].recv()
        wire["tfh", c].recv()

    def combine(c, g):
        for copy in load_c[c, g]:
            copy.wait()

        def step(zz, _):
            acc = None
            for p in range(2):
                for k in range(coils):
                    w = sb[c, g, p, k, zz].astype(F32)
                    vals = [cb[c, g, i, p, k, zz].astype(F32) * w for i in range(nf)] + [w * w]
                    acc = vals if acc is None else [x + v for x, v in zip(acc, vals)]
            z = per * g + zz
            xs = pl.ds(CHUNK * c, CHUNK)
            for i in range(nf):
                comb[i, z, xs, :] = acc[i]
            ener[z, xs, :] = acc[nf]
            return 0

        lax.fori_loop(0, per, step, 0)

    def tile(i):
        rbl = lax.div(i, ny // LANES)
        lh = lax.rem(i, ny // LANES)
        return rbl, pl.ds(pl.multiple_of(lh * LANES, LANES), LANES)

    def adjoint(c):
        def step(i, _):
            rbl, lanes = tile(i)
            rb = 2 * c + rbl
            rows = pl.ds(pl.multiple_of(rb * ROWS, ROWS), ROWS)
            sums = [None] * (planes + 2 * BOUND)
            for z in range(planes):
                en = ener[z, rows, lanes]
                for i_f in range(nf):
                    place = locate(dv[i_f, z, rows, lanes])
                    warped = gather_line(place, lambda j: tx[rb, z + j, :, lanes])
                    value = comb[i_f, z, rows, lanes] - en * warped
                    for j, term in enumerate(scatter_line(place, value)):
                        sums[z + j] = term if sums[z + j] is None else sums[z + j] + term
            for q, total in enumerate(sums):
                adj[rb, q, :, lanes] = total
            return 0

        lax.fori_loop(0, 2 * (ny // LANES), step, 0)

    def adj_mate(c):
        other = 2 * c + 1 - h
        wire["am", c] = Remote(adj.at[other], radj.at[c], to_mate)

    def adj_slab(c):
        rb = 2 * c + h
        wire["am", c].recv()
        for part in (low, high):
            adj[rb, part] = adj[rb, part] + radj[c, part]
        wire["au", c] = up(adj.at[rb, high], rlo.at[c])
        wire["ad", c] = down(adj.at[rb, low], rhi.at[c])
        csum[c] = adj[rb, own] + radj[c, own]

    def adj_across(c):
        wire["au", c].recv()
        wire["ad", c].recv()
        csum[c] = csum[c] + (rlo[c] + rhi[c])
        wire["ac", c] = Remote(csum.at[c], rc.at[c], to_across)

    def refresh(c):
        rb = 2 * c + h
        wire["ac", c].recv()
        rx[rb, own] = tx[rb, own] + (csum[c] + rc[c]) * (1.0 / frames_all)
        wire["rm", c] = Remote(rx.at[rb, own], rx.at[rb, own], to_mate)
        wire["ru", c] = up(rx.at[rb, own], rx.at[rb, low])
        wire["rd", c] = down(rx.at[rb, own], rx.at[rb, high])

    def refresh_pass(c):
        rb = 2 * c + h
        wire["ru", c].recv()
        wire["rd", c].recv()
        wire["rfl", c] = Remote(rx.at[rb, low], rx.at[rb, low], to_mate, has_below, has_below)
        wire["rfh", c] = Remote(rx.at[rb, high], rx.at[rb, high], to_mate, has_above, has_above)

    def refresh_in(c):
        wire["rm", c].recv()
        wire["rfl", c].recv()
        wire["rfh", c].recv()

    saves = []

    def save_template(b):
        saves.append(local(rx.at[b, own], out_t.at[:, pl.ds(ROWS * b, ROWS), :]))

    def gradients(b):
        first = lax.broadcasted_iota(jnp.int32, (ROWS, ny), 0) == 0
        last = lax.broadcasted_iota(jnp.int32, (ROWS, ny), 0) == ROWS - 1
        left = lax.broadcasted_iota(jnp.int32, (ROWS, ny), 1) == 0
        right = lax.broadcasted_iota(jnp.int32, (ROWS, ny), 1) == ny - 1

        def step(z, _):
            here = rx[b, BOUND + z]
            down_edge = pltpu.roll(rx[b - 1, BOUND + z], 1, 0) if b > 0 else jnp.zeros_like(here)
            up_edge = pltpu.roll(rx[b + 1, BOUND + z], ROWS - 1, 0) if b < n_rb - 1 else jnp.zeros_like(here)
            prev_x = jnp.where(first, down_edge, pltpu.roll(here, 1, 0))
            next_x = jnp.where(last, up_edge, pltpu.roll(here, ROWS - 1, 0))
            prev_y = jnp.where(left, 0.0, pltpu.roll(here, 1, 1))
            next_y = jnp.where(right, 0.0, pltpu.roll(here, ny - 1, 1))
            gx = (next_x - prev_x) * 0.5
            gy = (next_y - prev_y) * 0.5
            g_z = (rx[b, BOUND + z + 1] - rx[b, BOUND + z - 1]) * 0.5
            gz[b, z] = g_z
            gs[b, z] = gx * gx + gy * gy + g_z * g_z
            return 0

        lax.fori_loop(0, planes, step, 0)

    def force(b):
        rows = pl.ds(b * ROWS, ROWS)

        def step(lh, _):
            lanes = pl.ds(pl.multiple_of(lh * LANES, LANES), LANES)
            for z in range(planes):
                for i_f in range(nf):
                    d = dv[i_f, z, rows, lanes]
                    warped = gather_line(locate(d), lambda j: rx[b, z + j, :, lanes])
                    miss = comb[i_f, z, rows, lanes] - warped
                    push = miss * gz[b, z, :, lanes] / (gs[b, z, :, lanes] + miss * miss + 1.0)
                    mv[i_f, RADIUS + z, rows, lanes] = d + push
            return 0

        lax.fori_loop(0, ny // LANES, step, 0)

    def moved_out(b):
        rows = pl.ds(b * ROWS, ROWS)
        head, tail = pl.ds(RADIUS, RADIUS), pl.ds(planes, RADIUS)
        wire["mu", b] = up(mv.at[:, tail, rows, :], mv.at[:, pl.ds(0, RADIUS), rows, :])
        wire["md", b] = down(mv.at[:, head, rows, :], mv.at[:, pl.ds(planes + RADIUS, RADIUS), rows, :])

    weights = [float(w) for w in gauss_weights()]

    def halves(value):
        hi = value.astype(BF16)
        return hi, (value - hi.astype(F32)).astype(BF16)

    def dot3(a_hi, a_lo, b_hi, b_lo):
        dot = functools.partial(jnp.dot, preferred_element_type=F32)
        return dot(a_hi, b_hi) + (dot(a_lo, b_hi) + dot(a_hi, b_lo))

    def smooth(i_f):
        def step(z, _):
            total = None
            for j in range(2 * RADIUS + 1):
                term = weights[j] * mv[i_f, z + j]
                total = term if total is None else total + term
            hi, lo = halves(total)
            at = pl.ds(pl.multiple_of(z * wide, wide), wide)
            shi[at, :] = hi
            slo[at, :] = lo
            return 0

        lax.fori_loop(0, planes, step, 0)
        along_y = dot3(shi[...], slo[...], ty_hi[...], ty_lo[...])
        y_hi, y_lo = halves(along_y)
        done = dot3(kx_hi[...], kx_lo[...], y_hi, y_lo)
        obuf[i_f] = (BOUND * jnp.tanh(done * (1.0 / BOUND))).reshape(planes, wide, ny)
        saves.append(local(obuf.at[i_f], out_d.at[i_f]))

    for copy in load_t:
        copy.wait()
    for c in range(n_chunk):
        template_out(c)
    zero_edges([(tx, slice(None), slice(0, BOUND)), (rx, slice(None), slice(0, BOUND)), (rlo,),
                (mv, slice(None), slice(0, RADIUS))],
               [(tx, slice(None), slice(BOUND + planes, None)), (rx, slice(None), slice(BOUND + planes, None)),
                (rhi,), (mv, slice(None), slice(planes + RADIUS, None))])
    combine(0, 0)
    combine(0, 1)
    template_pass(0)
    combine(0, 2)
    template_pass(1)
    combine(0, 3)
    load_d.wait()
    template_in(0)
    adjoint(0)
    adj_mate(0)
    combine(1, 0)
    adj_slab(0)
    combine(1, 1)
    combine(1, 2)
    adj_across(0)
    combine(1, 3)
    template_in(1)
    adjoint(1)
    adj_mate(1)
    refresh(0)
    adj_slab(1)
    refresh_pass(0)
    adj_across(1)
    refresh_in(0)
    save_template(0)
    save_template(1)
    gradients(0)
    force(0)
    moved_out(0)
    refresh(1)
    refresh_pass(1)
    refresh_in(1)
    save_template(2)
    save_template(3)
    for b in range(1, n_rb):
        gradients(b)
        force(b)
        moved_out(b)
    for copy in load_k:
        copy.wait()
    for b in range(n_rb):
        wire["mu", b].recv()
        wire["md", b].recv()
    for i_f in range(nf):
        smooth(i_f)
    for item in pending:
        item.sent()
    for copy in saves:
        copy.wait()


def per_device(template, displacement, coil_images, sensitivities):
    nf, planes, wide, ny = displacement.shape
    coils = coil_images.shape[2]
    n_slab = lax.axis_size("slab")
    n_frame = lax.axis_size("frame")
    n_rb, n_chunk, per = wide // ROWS, wide // CHUNK, planes // GROUPS
    deep = planes + 2 * BOUND
    ty_hi, ty_lo = split_table(gauss_table(ny))
    kx_hi, kx_lo = split_table(np.kron(np.eye(planes), gauss_table(wide)))
    side = planes * wide
    any_ = pl.BlockSpec(memory_space=pl.ANY)
    scratch = [
        pltpu.VMEM((n_rb, deep, ROWS, ny), F32),
        pltpu.VMEM((n_rb, deep, ROWS, ny), F32),
        pltpu.VMEM((nf, planes, wide, ny), F32),
        pltpu.VMEM((n_chunk, GROUPS, nf, 2, coils, per, CHUNK, ny), BF16),
        pltpu.VMEM((n_chunk, GROUPS, 2, coils, per, CHUNK, ny), BF16),
        pltpu.VMEM((nf, planes, wide, ny), F32),
        pltpu.VMEM((planes, wide, ny), F32),
        pltpu.VMEM((n_rb, deep, ROWS, ny), F32),
        pltpu.VMEM((n_chunk, deep, ROWS, ny), F32),
        pltpu.VMEM((n_chunk, BOUND, ROWS, ny), F32),
        pltpu.VMEM((n_chunk, BOUND, ROWS, ny), F32),
        pltpu.VMEM((n_chunk, planes, ROWS, ny), F32),
        pltpu.VMEM((n_chunk, planes, ROWS, ny), F32),
        pltpu.VMEM((nf, planes + 2 * RADIUS, wide, ny), F32),
        pltpu.VMEM((n_rb, planes, ROWS, ny), F32),
        pltpu.VMEM((n_rb, planes, ROWS, ny), F32),
        pltpu.VMEM((side, ny), BF16),
        pltpu.VMEM((side, ny), BF16),
        pltpu.VMEM((nf, planes, wide, ny), F32),
        pltpu.VMEM((ny, ny), BF16),
        pltpu.VMEM((ny, ny), BF16),
        pltpu.VMEM((side, side), BF16),
        pltpu.VMEM((side, side), BF16),
        pltpu.SemaphoreType.DMA((48,)),
        pltpu.SemaphoreType.DMA((40,)),
        pltpu.SemaphoreType.DMA((40,)),
    ]
    return pl.pallas_call(
        functools.partial(kernel, (n_slab, nf * n_frame, coils)),
        out_shape=(
            jax.ShapeDtypeStruct((planes, wide, ny), F32),
            jax.ShapeDtypeStruct((nf, planes, wide, ny), F32),
        ),
        in_specs=[any_] * 8,
        out_specs=(any_, any_),
        scratch_shapes=scratch,
        compiler_params=pltpu.CompilerParams(
            collective_id=0, has_side_effects=True, vmem_limit_bytes=50 * 1024 * 1024
        ),
        cost_estimate=pl.CostEstimate(flops=10**8, bytes_accessed=2 * 10**7, transcendentals=0),
    )(template, displacement, coil_images, sensitivities,
      jnp.asarray(ty_hi), jnp.asarray(ty_lo), jnp.asarray(kx_hi), jnp.asarray(kx_lo))


def solution(mesh):
    placed = (
        P("slab", None, None),
        P("frame", "slab", None, None),
        P("frame", None, None, "slab", None, None),
        P(None, None, "slab", None, None),
    )
    return jax.shard_map(
        per_device,
        mesh=mesh,
        in_specs=placed,
        out_specs=(P("slab", None, None), P("frame", "slab", None, None)),
        check_vma=False,
    )
```

```python
import functools

import jax
import jax.numpy as jnp
import numpy as np
from jax import lax
from jax.experimental import pallas as pl
from jax.experimental.pallas import tpu as pltpu
from jax.sharding import PartitionSpec as P

BOUND = 8
RADIUS = 4
ROWS = 8
LANES = 128
CHUNK = 16
GROUPS = 4
MESH = pl.DeviceIdType.MESH
F32 = jnp.float32
BF16 = jnp.bfloat16


def gauss_weights():
    j = np.arange(-RADIUS, RADIUS + 1, dtype=np.float64)
    spread = RADIUS * 0.5
    w = np.exp(-j * j / (2.0 * spread * spread))
    return w / w.sum()


def gauss_table(length):
    w = gauss_weights()
    table = np.zeros((length, length), np.float64)
    for j in range(-RADIUS, RADIUS + 1):
        table += w[j + RADIUS] * np.eye(length, k=j)
    return table


def split_table(table):
    hi = table.astype(np.float32).astype(BF16)
    lo = (table - hi.astype(np.float64)).astype(np.float32).astype(BF16)
    return hi, lo


def locate(d):
    m3 = d >= 0.0
    r = jnp.where(m3, d, d + 8.0)
    m2 = r >= 4.0
    r = jnp.where(m2, r - 4.0, r)
    m1 = r >= 2.0
    r = jnp.where(m1, r - 2.0, r)
    m0 = r >= 1.0
    t = jnp.where(m0, r - 1.0, r)
    return m3, m2, m1, m0, t


def gather_line(place, plane):
    m3, m2, m1, m0, t = place
    a = [plane(j) for j in range(17)]
    b = [jnp.where(m3, a[j + 8], a[j]) for j in range(9)]
    c = [jnp.where(m2, b[j + 4], b[j]) for j in range(5)]
    e = [jnp.where(m1, c[j + 2], c[j]) for j in range(3)]
    lo = jnp.where(m0, e[1], e[0])
    hi = jnp.where(m0, e[2], e[1])
    return lo + t * (hi - lo)


def scatter_line(place, value):
    m3, m2, m1, m0, t = place
    hi = t * value
    lo = value - hi
    zero = jnp.zeros_like(value)
    e = [jnp.where(m0, zero, lo), jnp.where(m0, lo, hi), jnp.where(m0, hi, zero)]

    def spread(src, mask, step):
        n = len(src)
        out = []
        for j in range(n + step):
            low = src[j] if j < n else zero
            high = src[j - step] if j >= step else zero
            out.append(jnp.where(mask, high, low))
        return out

    return spread(spread(spread(e, m1, 2), m2, 4), m3, 8)


def kernel(cfg, tmpl, disp, coil, sens, ty_hi_h, ty_lo_h, kx_hi_h, kx_lo_h, out_t, out_d,
           tx, rx, dv, cb, sb, comb, ener, adj, radj, ra, mv,
           shi, slo, obuf, ty_hi, ty_lo, kx_hi, kx_lo, lsem, ssem, rsem):
    n_slab, frames_all, coils = cfg
    nf, planes, wide, ny = obuf.shape
    n_rb = wide // ROWS
    n_lh = ny // LANES
    n_chunk = wide // CHUNK
    per = planes // GROUPS
    reach = BOUND + RADIUS
    f = lax.axis_index("frame")
    s = lax.axis_index("slab")
    h = lax.rem(f, 2)
    q = lax.div(f, 2)
    o = 1 - q
    mate = f + 1 - 2 * h
    across = f + 2 - 4 * q
    at_slab = {k: lax.rem(s + k + n_slab, n_slab) for k in (-2, -1, 0, 1, 2)}
    exists = {-2: s > 1, -1: s > 0, 0: None, 1: s < n_slab - 1, 2: s < n_slab - 2}

    counter = [0]

    def local(src, dst):
        copy = pltpu.make_async_copy(src, dst, lsem.at[counter[0]])
        counter[0] += 1
        copy.start()
        return copy

    load_t = [local(tmpl.at[:, pl.ds(ROWS * b, ROWS), pl.ds(LANES * l, LANES)], tx.at[b, l, pl.ds(BOUND, planes)])
              for b in range(n_rb) for l in range(n_lh)]
    load_d = local(disp, dv.at[:, pl.ds(RADIUS, planes)])
    load_c = {}
    for c in range(n_chunk):
        for g in range(GROUPS):
            zs, xs = pl.ds(per * g, per), pl.ds(CHUNK * c, CHUNK)
            load_c[c, g] = (
                local(sens.at[:, :, zs, xs, :], sb.at[c, g]),
                local(coil.at[:, :, :, zs, xs, :], cb.at[c, g]),
            )
    load_k = [local(a, b) for a, b in ((ty_hi_h, ty_hi), (ty_lo_h, ty_lo), (kx_hi_h, kx_hi), (kx_lo_h, kx_lo))]

    def clear(ref, *index):
        ref[index] = jnp.zeros_like(ref[index])

    every = slice(None)

    @pl.when(s == 0)
    def _():
        clear(tx, every, every, slice(0, BOUND))
        clear(rx, every, every, slice(0, reach))
        clear(dv, every, slice(0, RADIUS))
        clear(comb, every, slice(0, RADIUS))

    @pl.when(s == 1)
    def _():
        clear(rx, every, every, slice(0, RADIUS))

    @pl.when(s == n_slab - 2)
    def _():
        clear(rx, every, every, slice(planes + reach + BOUND, None))

    @pl.when(s == n_slab - 1)
    def _():
        clear(tx, every, every, slice(BOUND + planes, None))
        clear(rx, every, every, slice(planes + reach, None))
        clear(dv, every, slice(planes + RADIUS, None))
        clear(comb, every, slice(planes + RADIUS, None))

    barrier = pltpu.get_barrier_semaphore()
    near = ((mate, s), (across, s), (f, at_slab[1]), (f, at_slab[-1]))
    for dev in near:
        pl.semaphore_signal(barrier, inc=1, device_id=dev, device_id_type=MESH)
    pl.semaphore_wait(barrier, len(near))

    rcount = [0]
    pending = []

    def maybe(condition, action):
        if condition is None:
            action()
        else:
            pl.when(condition)(action)

    class Remote:
        def __init__(self, src, dst, frame, step=0):
            n = rcount[0]
            rcount[0] += 1
            self.copy = pltpu.make_async_remote_copy(
                src_ref=src, dst_ref=dst, send_sem=ssem.at[n], recv_sem=rsem.at[n],
                device_id=(frame, at_slab[step]), device_id_type=MESH)
            self.send_if, self.recv_if = exists[step], exists[-step]
            maybe(self.send_if, lambda: self.copy.start())
            pending.append(self)

        def recv(self):
            maybe(self.recv_if, lambda: self.copy.wait_recv())

        def sent(self):
            maybe(self.send_if, lambda: self.copy.wait_send())

    own = pl.ds(BOUND, planes)
    low = pl.ds(0, BOUND)
    high = pl.ds(BOUND + planes, BOUND)
    inner = pl.ds(reach, planes)
    wire = {}

    def arrive(*keys):
        for key in keys:
            for item in wire[key]:
                item.recv()

    def template_out(c):
        rb = 2 * c + h
        wire["t", c] = [Remote(tx.at[rb, :, own], tx.at[rb, :, low], f, 1),
                        Remote(tx.at[rb, :, own], tx.at[rb, :, high], f, -1)]

    def template_pass(c):
        rb = 2 * c + h
        arrive(("t", c))
        wire["tf", c] = [Remote(tx.at[rb, :, part], tx.at[rb, :, part], mate) for part in (low, high)]

    def template_in(c):
        arrive(("tf", c))

    def disp_out():
        wire["d"] = [
            Remote(dv.at[:, pl.ds(planes, RADIUS)], dv.at[:, pl.ds(0, RADIUS)], f, 1),
            Remote(dv.at[:, pl.ds(RADIUS, RADIUS)], dv.at[:, pl.ds(planes + RADIUS, RADIUS)], f, -1)]

    def comb_out(c):
        xs = pl.ds(CHUNK * c, CHUNK)
        wire["c", c] = [
            Remote(comb.at[:, pl.ds(planes, RADIUS), xs], comb.at[:, pl.ds(0, RADIUS), xs], f, 1),
            Remote(comb.at[:, pl.ds(RADIUS, RADIUS), xs], comb.at[:, pl.ds(planes + RADIUS, RADIUS), xs], f, -1)]

    def combine(c, g):
        for copy in load_c[c, g]:
            copy.wait()

        def step(zz, _):
            acc = None
            for p in range(2):
                for k in range(coils):
                    w = sb[c, g, p, k, zz].astype(F32)
                    vals = [cb[c, g, i, p, k, zz].astype(F32) * w for i in range(nf)] + [w * w]
                    acc = vals if acc is None else [x + v for x, v in zip(acc, vals)]
            z = per * g + zz
            xs = pl.ds(CHUNK * c, CHUNK)
            for i in range(nf):
                comb[i, RADIUS + z, xs, :] = acc[i]
            ener[z, xs, :] = acc[nf]
            return 0

        lax.fori_loop(0, per, step, 0)

    def adjoint(c):
        def step(i, _):
            l = lax.rem(i, n_lh)
            rb = 2 * c + lax.div(i, n_lh)
            lanes = pl.ds(pl.multiple_of(l * LANES, LANES), LANES)
            rows = pl.ds(pl.multiple_of(rb * ROWS, ROWS), ROWS)
            sums = [None] * (planes + 2 * BOUND)
            for z in range(planes):
                en = ener[z, rows, lanes]
                for i_f in range(nf):
                    place = locate(dv[i_f, RADIUS + z, rows, lanes])
                    warped = gather_line(place, lambda j: tx[rb, l, z + j])
                    value = comb[i_f, RADIUS + z, rows, lanes] - en * warped
                    for j, term in enumerate(scatter_line(place, value)):
                        sums[z + j] = term if sums[z + j] is None else sums[z + j] + term
            for at, total in enumerate(sums):
                adj[rb, l, at] = total
            return 0

        lax.fori_loop(0, 2 * n_lh, step, 0)

    def adj_mate(c):
        wire["am", c] = [Remote(adj.at[2 * c + 1 - h], radj.at[c], mate)]

    def adj_out(c):
        rb = 2 * c + h
        arrive(("am", c))
        for part in (high, low):
            adj[rb, o, part] = adj[rb, o, part] + radj[c, o, part]
        sends = [Remote(adj.at[rb, o, high], ra.at[c, 0], across, 1),
                 Remote(adj.at[rb, o, low], ra.at[c, 1], across, -1)]
        for part in (high, low):
            adj[rb, q, part] = adj[rb, q, part] + radj[c, q, part]
        sends += [Remote(adj.at[rb, q, high], ra.at[c, 2], f, 1),
                  Remote(adj.at[rb, q, low], ra.at[c, 3], f, -1)]
        adj[rb, o, own] = adj[rb, o, own] + radj[c, o, own]
        sends += [Remote(adj.at[rb, o, own], ra.at[c, 4], across)]
        adj[rb, q, own] = adj[rb, q, own] + radj[c, q, own]
        wire["a", c] = sends

    def refresh(c):
        rb = 2 * c + h
        arrive(("a", c))

        total = adj[rb, q, own] + ra[c, 4]
        for up, sides in ((True, (0, 2)), (False, (1, 3))):
            for k in sides:
                ok = exists[-1] if up else exists[1]
                total = total + jnp.where(ok, ra[c, k], 0.0)
        rx[rb, q, inner] = tx[rb, q, own] + total * (1.0 / frames_all)
        mine = rx.at[rb, q]
        tail, head = mine.at[pl.ds(reach + RADIUS, RADIUS)], mine.at[pl.ds(reach, RADIUS)]
        whole = mine.at[inner]
        sends = []
        for frame in (across, f):
            sends += [Remote(tail, mine.at[pl.ds(0, RADIUS)], frame, 2),
                      Remote(head, mine.at[pl.ds(planes + reach + BOUND, RADIUS)], frame, -2)]
        for frame in (across, f):
            sends += [Remote(whole, mine.at[pl.ds(RADIUS, BOUND)], frame, 1),
                      Remote(whole, mine.at[pl.ds(planes + reach, BOUND)], frame, -1)]
        sends += [Remote(whole, whole, across)]
        wire["r", c] = sends

    def refresh_pass(c):
        rb = 2 * c + h
        arrive(("r", c))
        wire["rf", c] = [Remote(rx.at[rb], rx.at[rb], mate)]

    def refresh_in(c):
        arrive(("rf", c))

    saves = []

    def save_template(b):
        for l in range(n_lh):
            saves.append(local(rx.at[b, l, inner], out_t.at[:, pl.ds(ROWS * b, ROWS), pl.ds(LANES * l, LANES)]))

    deep = planes + 2 * RADIUS
    UNROLL = 4

    def mismatch(c):
        def step(i, _):
            col = lax.div(i, deep // UNROLL)
            base = lax.rem(i, deep // UNROLL) * UNROLL
            l = lax.rem(col, n_lh)
            rb = 2 * c + lax.div(col, n_lh)
            lanes = pl.ds(pl.multiple_of(l * LANES, LANES), LANES)
            rows = pl.ds(pl.multiple_of(rb * ROWS, ROWS), ROWS)
            for k in range(UNROLL):
                p = base + k
                for i_f in range(nf):
                    warped = gather_line(locate(dv[i_f, p, rows, lanes]), lambda j: rx[rb, l, p + j])
                    mv[i_f, p, rows, lanes] = comb[i_f, p, rows, lanes] - warped
            return 0

        lax.fori_loop(0, 2 * n_lh * (deep // UNROLL), step, 0)

    def push(b):
        row = lax.broadcasted_iota(jnp.int32, (ROWS, LANES), 0)
        lane = lax.broadcasted_iota(jnp.int32, (ROWS, LANES), 1)
        first, last = row == 0, row == ROWS - 1
        left, right = lane == 0, lane == LANES - 1
        rows = pl.ds(b * ROWS, ROWS)
        zero = jnp.zeros((ROWS, LANES), F32)

        def step(i, _):
            for k in range(UNROLL):
                p = i * UNROLL + k
                at = p + BOUND
                for l in range(n_lh):
                    lanes = pl.ds(l * LANES, LANES)
                    here = rx[b, l, at]
                    before = pltpu.roll(rx[b - 1, l, at], 1, 0) if b > 0 else zero
                    after = pltpu.roll(rx[b + 1, l, at], ROWS - 1, 0) if b < n_rb - 1 else zero
                    prev_x = jnp.where(first, before, pltpu.roll(here, 1, 0))
                    next_x = jnp.where(last, after, pltpu.roll(here, ROWS - 1, 0))
                    before = pltpu.roll(rx[b, l - 1, at], 1, 1) if l > 0 else zero
                    after = pltpu.roll(rx[b, l + 1, at], LANES - 1, 1) if l < n_lh - 1 else zero
                    prev_y = jnp.where(left, before, pltpu.roll(here, 1, 1))
                    next_y = jnp.where(right, after, pltpu.roll(here, LANES - 1, 1))
                    gx = (next_x - prev_x) * 0.5
                    gy = (next_y - prev_y) * 0.5
                    gz = (rx[b, l, at + 1] - rx[b, l, at - 1]) * 0.5
                    floor = gx * gx + gy * gy + gz * gz + 1.0
                    for i_f in range(nf):
                        miss = mv[i_f, p, rows, lanes]
                        mv[i_f, p, rows, lanes] = dv[i_f, p, rows, lanes] + miss * gz / (floor + miss * miss)
            return 0

        lax.fori_loop(0, deep // UNROLL, step, 0)

    weights = [float(w) for w in gauss_weights()]

    def halves(value):
        hi = value.astype(BF16)
        return hi, (value - hi.astype(F32)).astype(BF16)

    def dot3(a_hi, a_lo, b_hi, b_lo):
        dot = functools.partial(jnp.dot, preferred_element_type=F32)
        return dot(a_hi, b_hi) + (dot(a_lo, b_hi) + dot(a_hi, b_lo))

    def smooth(i_f):
        for z in range(planes):
            total = None
            for j in range(2 * RADIUS + 1):
                term = weights[j] * mv[i_f, z + j]
                total = term if total is None else total + term
            hi, lo = halves(total)
            at = pl.ds(z * wide, wide)
            shi[at, :] = hi
            slo[at, :] = lo
        along_y = dot3(shi[...], slo[...], ty_hi[...], ty_lo[...])
        y_hi, y_lo = halves(along_y)
        done = dot3(kx_hi[...], kx_lo[...], y_hi, y_lo)
        obuf[i_f] = (BOUND * jnp.tanh(done * (1.0 / BOUND))).reshape(planes, wide, ny)
        saves.append(local(obuf.at[i_f], out_d.at[i_f]))

    for copy in load_t:
        copy.wait()
    for c in range(n_chunk):
        template_out(c)
    for g in range(GROUPS):
        combine(0, g)
    load_d.wait()
    disp_out()
    combine(1, 0)
    combine(1, 1)
    template_pass(0)
    combine(1, 2)
    combine(1, 3)
    template_pass(1)
    template_in(0)
    adjoint(0)
    adj_mate(0)
    template_in(1)
    adjoint(1)
    adj_mate(1)
    adj_out(0)
    adj_out(1)
    comb_out(0)
    comb_out(1)
    refresh(0)
    refresh(1)
    for copy in load_k:
        copy.wait()
    refresh_pass(0)
    refresh_pass(1)
    arrive("d", ("c", 0), ("c", 1))
    refresh_in(0)
    mismatch(0)
    push(0)
    save_template(0)
    save_template(1)
    refresh_in(1)
    save_template(2)
    save_template(3)
    mismatch(1)
    for b in range(1, n_rb):
        push(b)

    @pl.when(s == 0)
    def _():
        clear(mv, every, slice(0, RADIUS))

    @pl.when(s == n_slab - 1)
    def _():
        clear(mv, every, slice(planes + RADIUS, None))

    for i_f in range(nf):
        smooth(i_f)
    for item in pending:
        item.sent()
    for copy in saves:
        copy.wait()


def per_device(template, displacement, coil_images, sensitivities):
    nf, planes, wide, ny = displacement.shape
    coils = coil_images.shape[2]
    n_slab = lax.axis_size("slab")
    n_frame = lax.axis_size("frame")
    n_rb, n_lh, n_chunk, per = wide // ROWS, ny // LANES, wide // CHUNK, planes // GROUPS
    ty_hi, ty_lo = split_table(gauss_table(ny))
    kx_hi, kx_lo = split_table(np.kron(np.eye(planes), gauss_table(wide)))
    side = planes * wide
    any_ = pl.BlockSpec(memory_space=pl.ANY)

    def columns(lead, depth):
        return pltpu.VMEM((*lead, depth, ROWS, LANES), F32)

    def field(depth):
        return pltpu.VMEM((nf, depth, wide, ny), F32)

    scratch = [
        columns((n_rb, n_lh), planes + 2 * BOUND),
        columns((n_rb, n_lh), planes + 2 * BOUND + 2 * RADIUS),
        field(planes + 2 * RADIUS),
        pltpu.VMEM((n_chunk, GROUPS, nf, 2, coils, per, CHUNK, ny), BF16),
        pltpu.VMEM((n_chunk, GROUPS, 2, coils, per, CHUNK, ny), BF16),
        field(planes + 2 * RADIUS),
        pltpu.VMEM((planes, wide, ny), F32),
        columns((n_rb, n_lh), planes + 2 * BOUND),
        columns((n_chunk, n_lh), planes + 2 * BOUND),
        columns((n_chunk, 5), planes),
        field(planes + 2 * RADIUS),
        pltpu.VMEM((side, ny), BF16),
        pltpu.VMEM((side, ny), BF16),
        field(planes),
        pltpu.VMEM((ny, ny), BF16),
        pltpu.VMEM((ny, ny), BF16),
        pltpu.VMEM((side, side), BF16),
        pltpu.VMEM((side, side), BF16),
        pltpu.SemaphoreType.DMA((48,)),
        pltpu.SemaphoreType.DMA((56,)),
        pltpu.SemaphoreType.DMA((56,)),
    ]
    return pl.pallas_call(
        functools.partial(kernel, (n_slab, nf * n_frame, coils)),
        out_shape=(
            jax.ShapeDtypeStruct((planes, wide, ny), F32),
            jax.ShapeDtypeStruct((nf, planes, wide, ny), F32),
        ),
        in_specs=[any_] * 8,
        out_specs=(any_, any_),
        scratch_shapes=scratch,
        compiler_params=pltpu.CompilerParams(
            collective_id=0, has_side_effects=True, vmem_limit_bytes=62 * 1024 * 1024
        ),
        cost_estimate=pl.CostEstimate(flops=10**8, bytes_accessed=2 * 10**7, transcendentals=0),
    )(template, displacement, coil_images, sensitivities,
      jnp.asarray(ty_hi), jnp.asarray(ty_lo), jnp.asarray(kx_hi), jnp.asarray(kx_lo))


def solution(mesh):
    placed = (
        P("slab", None, None),
        P("frame", "slab", None, None),
        P("frame", None, None, "slab", None, None),
        P(None, None, "slab", None, None),
    )
    return jax.shard_map(
        per_device,
        mesh=mesh,
        in_specs=placed,
        out_specs=(P("slab", None, None), P("frame", "slab", None, None)),
        check_vma=False,
    )
```

```python
import functools

import jax
import jax.numpy as jnp
import numpy as np
from jax import lax
from jax.experimental import pallas as pl
from jax.experimental.pallas import tpu as pltpu
from jax.sharding import PartitionSpec as P

BOUND = 8
RADIUS = 4
ROWS = 8
LANES = 128
CHUNK = 16
GROUPS = 4
MESH = pl.DeviceIdType.MESH
F32 = jnp.float32
BF16 = jnp.bfloat16


def gauss_weights():
    j = np.arange(-RADIUS, RADIUS + 1, dtype=np.float64)
    spread = RADIUS * 0.5
    w = np.exp(-j * j / (2.0 * spread * spread))
    return w / w.sum()


def gauss_table(length):
    w = gauss_weights()
    table = np.zeros((length, length), np.float64)
    for j in range(-RADIUS, RADIUS + 1):
        table += w[j + RADIUS] * np.eye(length, k=j)
    return table


def split_table(table):
    hi = table.astype(np.float32).astype(BF16)
    lo = (table - hi.astype(np.float64)).astype(np.float32).astype(BF16)
    return hi, lo


def locate(d):
    m3 = d >= 0.0
    r = jnp.where(m3, d, d + 8.0)
    m2 = r >= 4.0
    r = jnp.where(m2, r - 4.0, r)
    m1 = r >= 2.0
    r = jnp.where(m1, r - 2.0, r)
    m0 = r >= 1.0
    t = jnp.where(m0, r - 1.0, r)
    return m3, m2, m1, m0, t


def gather_line(place, plane):
    m3, m2, m1, m0, t = place
    a = [plane(j) for j in range(17)]
    b = [jnp.where(m3, a[j + 8], a[j]) for j in range(9)]
    c = [jnp.where(m2, b[j + 4], b[j]) for j in range(5)]
    e = [jnp.where(m1, c[j + 2], c[j]) for j in range(3)]
    lo = jnp.where(m0, e[1], e[0])
    hi = jnp.where(m0, e[2], e[1])
    return lo + t * (hi - lo)


def scatter_line(place, value):
    m3, m2, m1, m0, t = place
    hi = t * value
    lo = value - hi
    zero = jnp.zeros_like(value)
    e = [jnp.where(m0, zero, lo), jnp.where(m0, lo, hi), jnp.where(m0, hi, zero)]

    def spread(src, mask, step):
        n = len(src)
        out = []
        for j in range(n + step):
            low = src[j] if j < n else zero
            high = src[j - step] if j >= step else zero
            out.append(jnp.where(mask, high, low))
        return out

    return spread(spread(spread(e, m1, 2), m2, 4), m3, 8)


def kernel(cfg, tmpl, disp, coil, sens, ty_hi_h, ty_lo_h, kx_hi_h, kx_lo_h, out_t, out_d,
           tx, rx, dv, cb, sb, comb, ener, adj, radj, ra, mv,
           shi, slo, obuf, ty_hi, ty_lo, kx_hi, kx_lo, lsem, ssem, rsem):
    n_slab, frames_all, coils = cfg
    nf, planes, wide, ny = obuf.shape
    n_rb = wide // ROWS
    n_lh = ny // LANES
    n_chunk = wide // CHUNK
    per = planes // GROUPS
    reach = BOUND + RADIUS
    f = lax.axis_index("frame")
    s = lax.axis_index("slab")
    h = lax.rem(f, 2)
    q = lax.div(f, 2)
    o = 1 - q
    mate = f + 1 - 2 * h
    across = f + 2 - 4 * q
    at_slab = {k: lax.rem(s + k + n_slab, n_slab) for k in (-2, -1, 0, 1, 2)}
    exists = {-2: s > 1, -1: s > 0, 0: None, 1: s < n_slab - 1, 2: s < n_slab - 2}

    counter = [0]

    def local(src, dst):
        copy = pltpu.make_async_copy(src, dst, lsem.at[counter[0]])
        counter[0] += 1
        copy.start()
        return copy

    load_t = [local(tmpl.at[:, pl.ds(ROWS * b, ROWS), pl.ds(LANES * l, LANES)], tx.at[b, l, pl.ds(BOUND, planes)])
              for b in range(n_rb) for l in range(n_lh)]
    load_d = local(disp, dv.at[:, pl.ds(RADIUS, planes)])
    load_c = {}
    for c in range(n_chunk):
        for g in range(GROUPS):
            zs, xs = pl.ds(per * g, per), pl.ds(CHUNK * c, CHUNK)
            load_c[c, g] = (
                local(sens.at[:, :, zs, xs, :], sb.at[c, g]),
                local(coil.at[:, :, :, zs, xs, :], cb.at[c, g]),
            )
    load_k = [local(a, b) for a, b in ((ty_hi_h, ty_hi), (ty_lo_h, ty_lo), (kx_hi_h, kx_hi), (kx_lo_h, kx_lo))]

    def clear(ref, *index):
        ref[index] = jnp.zeros_like(ref[index])

    every = slice(None)

    @pl.when(s == 0)
    def _():
        clear(tx, every, every, slice(0, BOUND))
        clear(rx, every, every, slice(0, reach))
        clear(dv, every, slice(0, RADIUS))
        clear(comb, every, slice(0, RADIUS))

    @pl.when(s == 1)
    def _():
        clear(rx, every, every, slice(0, RADIUS))

    @pl.when(s == n_slab - 2)
    def _():
        clear(rx, every, every, slice(planes + reach + BOUND, None))

    @pl.when(s == n_slab - 1)
    def _():
        clear(tx, every, every, slice(BOUND + planes, None))
        clear(rx, every, every, slice(planes + reach, None))
        clear(dv, every, slice(planes + RADIUS, None))
        clear(comb, every, slice(planes + RADIUS, None))

    barrier = pltpu.get_barrier_semaphore()
    near = ((mate, s), (across, s), (f, at_slab[1]), (f, at_slab[-1]))
    for dev in near:
        pl.semaphore_signal(barrier, inc=1, device_id=dev, device_id_type=MESH)
    pl.semaphore_wait(barrier, len(near))

    rcount = [0]
    pending = []

    def maybe(condition, action):
        if condition is None:
            action()
        else:
            pl.when(condition)(action)

    class Remote:
        def __init__(self, src, dst, frame, step=0):
            n = rcount[0]
            rcount[0] += 1
            self.copy = pltpu.make_async_remote_copy(
                src_ref=src, dst_ref=dst, send_sem=ssem.at[n], recv_sem=rsem.at[n],
                device_id=(frame, at_slab[step]), device_id_type=MESH)
            self.send_if, self.recv_if = exists[step], exists[-step]
            maybe(self.send_if, lambda: self.copy.start())
            pending.append(self)

        def recv(self):
            maybe(self.recv_if, lambda: self.copy.wait_recv())

        def sent(self):
            maybe(self.send_if, lambda: self.copy.wait_send())

    own = pl.ds(BOUND, planes)
    low = pl.ds(0, BOUND)
    high = pl.ds(BOUND + planes, BOUND)
    inner = pl.ds(reach, planes)
    wire = {}

    def arrive(*keys):
        for key in keys:
            for item in wire[key]:
                item.recv()

    def template_out(c):
        rb = 2 * c + h
        wire["t", c] = [Remote(tx.at[rb, :, own], tx.at[rb, :, low], f, 1),
                        Remote(tx.at[rb, :, own], tx.at[rb, :, high], f, -1)]

    def template_pass(c):
        rb = 2 * c + h
        arrive(("t", c))
        wire["tf", c] = [Remote(tx.at[rb, :, part], tx.at[rb, :, part], mate) for part in (low, high)]

    def template_in(c):
        arrive(("tf", c))

    def disp_out():
        wire["d"] = [
            Remote(dv.at[:, pl.ds(planes, RADIUS)], dv.at[:, pl.ds(0, RADIUS)], f, 1),
            Remote(dv.at[:, pl.ds(RADIUS, RADIUS)], dv.at[:, pl.ds(planes + RADIUS, RADIUS)], f, -1)]

    def comb_out(c):
        xs = pl.ds(CHUNK * c, CHUNK)
        wire["c", c] = [
            Remote(comb.at[:, pl.ds(planes, RADIUS), xs], comb.at[:, pl.ds(0, RADIUS), xs], f, 1),
            Remote(comb.at[:, pl.ds(RADIUS, RADIUS), xs], comb.at[:, pl.ds(planes + RADIUS, RADIUS), xs], f, -1)]

    def combine(c, g):
        for copy in load_c[c, g]:
            copy.wait()

        def step(zz, _):
            acc = None
            for p in range(2):
                for k in range(coils):
                    w = sb[c, g, p, k, zz].astype(F32)
                    vals = [cb[c, g, i, p, k, zz].astype(F32) * w for i in range(nf)] + [w * w]
                    acc = vals if acc is None else [x + v for x, v in zip(acc, vals)]
            z = per * g + zz
            xs = pl.ds(CHUNK * c, CHUNK)
            for i in range(nf):
                comb[i, RADIUS + z, xs, :] = acc[i]
            ener[z, xs, :] = acc[nf]
            return 0

        lax.fori_loop(0, per, step, 0)

    def adjoint(c):
        def step(i, _):
            l = lax.rem(i, n_lh)
            rb = 2 * c + lax.div(i, n_lh)
            lanes = pl.ds(pl.multiple_of(l * LANES, LANES), LANES)
            rows = pl.ds(pl.multiple_of(rb * ROWS, ROWS), ROWS)
            sums = [None] * (planes + 2 * BOUND)
            for z in range(planes):
                en = ener[z, rows, lanes]
                for i_f in range(nf):
                    place = locate(dv[i_f, RADIUS + z, rows, lanes])
                    warped = gather_line(place, lambda j: tx[rb, l, z + j])
                    value = comb[i_f, RADIUS + z, rows, lanes] - en * warped
                    for j, term in enumerate(scatter_line(place, value)):
                        sums[z + j] = term if sums[z + j] is None else sums[z + j] + term
            for at, total in enumerate(sums):
                adj[rb, l, at] = total
            return 0

        lax.fori_loop(0, 2 * n_lh, step, 0)

    def adj_mate(c):
        wire["am", c] = [Remote(adj.at[2 * c + 1 - h], radj.at[c], mate)]

    def adj_out(c):
        rb = 2 * c + h
        arrive(("am", c))
        for part in (high, low):
            adj[rb, o, part] = adj[rb, o, part] + radj[c, o, part]
        sends = [Remote(adj.at[rb, o, high], ra.at[c, 0], across, 1),
                 Remote(adj.at[rb, o, low], ra.at[c, 1], across, -1)]
        for part in (high, low):
            adj[rb, q, part] = adj[rb, q, part] + radj[c, q, part]
        sends += [Remote(adj.at[rb, q, high], ra.at[c, 2], f, 1),
                  Remote(adj.at[rb, q, low], ra.at[c, 3], f, -1)]
        adj[rb, o, own] = adj[rb, o, own] + radj[c, o, own]
        sends += [Remote(adj.at[rb, o, own], ra.at[c, 4], across)]
        adj[rb, q, own] = adj[rb, q, own] + radj[c, q, own]
        wire["a", c] = sends

    def refresh(c):
        rb = 2 * c + h
        arrive(("a", c))

        total = adj[rb, q, own] + ra[c, 4]
        for up, sides in ((True, (0, 2)), (False, (1, 3))):
            for k in sides:
                ok = exists[-1] if up else exists[1]
                total = total + jnp.where(ok, ra[c, k], 0.0)
        rx[rb, q, inner] = tx[rb, q, own] + total * (1.0 / frames_all)
        mine = rx.at[rb, q]
        whole = mine.at[inner]
        sends = []
        for frame in (across, f):
            sends += [Remote(whole, mine.at[pl.ds(RADIUS, BOUND)], frame, 1),
                      Remote(whole, mine.at[pl.ds(planes + reach, BOUND)], frame, -1)]
        sends += [Remote(whole, whole, across)]
        wire["r", c] = sends

    def far_out(c):
        mine = rx.at[2 * c + h, q]
        tail, head = mine.at[pl.ds(reach + RADIUS, RADIUS)], mine.at[pl.ds(reach, RADIUS)]
        wire["far", c] = []
        for frame in (across, f):
            wire["far", c] += [Remote(tail, mine.at[pl.ds(0, RADIUS)], frame, 2),
                               Remote(head, mine.at[pl.ds(planes + reach + BOUND, RADIUS)], frame, -2)]

    def refresh_pass(c):
        rb = 2 * c + h
        arrive(("r", c))
        near = rx.at[rb, :, pl.ds(RADIUS, planes + 2 * BOUND)]
        wire["rf", c] = [Remote(near, near, mate)]

    def refresh_in(c):
        arrive(("rf", c))

    def far_pass(c):
        rb = 2 * c + h
        arrive(("far", c))
        ends = [rx.at[rb, :, pl.ds(0, RADIUS)], rx.at[rb, :, pl.ds(planes + reach + BOUND, RADIUS)]]
        wire["ff", c] = [Remote(end, end, mate) for end in ends]

    def far_in(c):
        arrive(("ff", c))

    saves = []

    def save_template(b):
        for l in range(n_lh):
            saves.append(local(rx.at[b, l, inner], out_t.at[:, pl.ds(ROWS * b, ROWS), pl.ds(LANES * l, LANES)]))

    OWN, HALO = (RADIUS, RADIUS), (0, planes + RADIUS)

    def warp(c, group):
        first, apart = group

        def step(i, _):
            col = lax.div(i, 2)
            base = first + apart * lax.rem(i, 2)
            l = lax.rem(col, n_lh)
            rb = 2 * c + lax.div(col, n_lh)
            lanes = pl.ds(pl.multiple_of(l * LANES, LANES), LANES)
            rows = pl.ds(pl.multiple_of(rb * ROWS, ROWS), ROWS)
            for k in range(RADIUS):
                p = base + k
                for i_f in range(nf):
                    mv[i_f, p, rows, lanes] = gather_line(locate(dv[i_f, p, rows, lanes]), lambda j: rx[rb, l, p + j])
            return 0

        lax.fori_loop(0, 4 * n_lh, step, 0)

    def push(b, group):
        row = lax.broadcasted_iota(jnp.int32, (ROWS, LANES), 0)
        lane = lax.broadcasted_iota(jnp.int32, (ROWS, LANES), 1)
        first, last = row == 0, row == ROWS - 1
        left, right = lane == 0, lane == LANES - 1
        rows = pl.ds(b * ROWS, ROWS)
        zero = jnp.zeros((ROWS, LANES), F32)

        def step(i, _):
            for k in range(RADIUS):
                p = group[0] + i * group[1] + k
                at = p + BOUND
                for l in range(n_lh):
                    lanes = pl.ds(l * LANES, LANES)
                    here = rx[b, l, at]
                    before = pltpu.roll(rx[b - 1, l, at], 1, 0) if b > 0 else zero
                    after = pltpu.roll(rx[b + 1, l, at], ROWS - 1, 0) if b < n_rb - 1 else zero
                    prev_x = jnp.where(first, before, pltpu.roll(here, 1, 0))
                    next_x = jnp.where(last, after, pltpu.roll(here, ROWS - 1, 0))
                    before = pltpu.roll(rx[b, l - 1, at], 1, 1) if l > 0 else zero
                    after = pltpu.roll(rx[b, l + 1, at], LANES - 1, 1) if l < n_lh - 1 else zero
                    prev_y = jnp.where(left, before, pltpu.roll(here, 1, 1))
                    next_y = jnp.where(right, after, pltpu.roll(here, LANES - 1, 1))
                    gx = (next_x - prev_x) * 0.5
                    gy = (next_y - prev_y) * 0.5
                    gz = (rx[b, l, at + 1] - rx[b, l, at - 1]) * 0.5
                    floor = gx * gx + gy * gy + gz * gz + 1.0
                    for i_f in range(nf):
                        miss = comb[i_f, p, rows, lanes] - mv[i_f, p, rows, lanes]
                        mv[i_f, p, rows, lanes] = dv[i_f, p, rows, lanes] + miss * gz / (floor + miss * miss)
            return 0

        lax.fori_loop(0, 2, step, 0)

    weights = [float(w) for w in gauss_weights()]

    def halves(value):
        hi = value.astype(BF16)
        return hi, (value - hi.astype(F32)).astype(BF16)

    def dot3(a_hi, a_lo, b_hi, b_lo):
        dot = functools.partial(jnp.dot, preferred_element_type=F32)
        return dot(a_hi, b_hi) + (dot(a_lo, b_hi) + dot(a_hi, b_lo))

    def taps(i_f, z, inside):
        total = obuf[i_f, z] if not inside else None
        for j in range(2 * RADIUS + 1):
            if inside == (RADIUS <= z + j < planes + RADIUS):
                term = weights[j] * mv[i_f, z + j]
                total = term if total is None else total + term
        return total

    def smooth_own(i_f):
        for z in range(planes):
            obuf[i_f, z] = taps(i_f, z, True)

    def smooth(i_f):
        for z in range(planes):
            hi, lo = halves(taps(i_f, z, False))
            at = pl.ds(z * wide, wide)
            shi[at, :] = hi
            slo[at, :] = lo
        along_y = dot3(shi[...], slo[...], ty_hi[...], ty_lo[...])
        y_hi, y_lo = halves(along_y)
        done = dot3(kx_hi[...], kx_lo[...], y_hi, y_lo)
        obuf[i_f] = (BOUND * jnp.tanh(done * (1.0 / BOUND))).reshape(planes, wide, ny)
        saves.append(local(obuf.at[i_f], out_d.at[i_f]))

    for copy in load_t:
        copy.wait()
    for c in range(n_chunk):
        template_out(c)
    for g in range(GROUPS):
        combine(0, g)
    load_d.wait()
    disp_out()
    combine(1, 0)
    combine(1, 1)
    template_pass(0)
    combine(1, 2)
    combine(1, 3)
    template_pass(1)
    comb_out(0)
    template_in(0)
    adjoint(0)
    adj_mate(0)
    template_in(1)
    adjoint(1)
    adj_mate(1)
    adj_out(0)
    adj_out(1)
    refresh(0)
    refresh(1)
    far_out(0)
    far_out(1)
    comb_out(1)
    for copy in load_k:
        copy.wait()
    refresh_pass(0)
    refresh_pass(1)
    refresh_in(0)
    warp(0, OWN)
    push(0, OWN)
    save_template(0)
    save_template(1)
    refresh_in(1)
    warp(1, OWN)
    save_template(2)
    save_template(3)
    far_pass(0)
    for b in range(1, n_rb):
        push(b, OWN)
    far_pass(1)
    for i_f in range(nf):
        smooth_own(i_f)
    arrive("d")
    far_in(0)
    warp(0, HALO)
    far_in(1)
    warp(1, HALO)
    arrive(("c", 0), ("c", 1))
    for b in range(n_rb):
        push(b, HALO)

    @pl.when(s == 0)
    def _():
        clear(mv, every, slice(0, RADIUS))

    @pl.when(s == n_slab - 1)
    def _():
        clear(mv, every, slice(planes + RADIUS, None))

    for i_f in range(nf):
        smooth(i_f)
    for item in pending:
        item.sent()
    for copy in saves:
        copy.wait()


def per_device(template, displacement, coil_images, sensitivities):
    nf, planes, wide, ny = displacement.shape
    coils = coil_images.shape[2]
    n_slab = lax.axis_size("slab")
    n_frame = lax.axis_size("frame")
    n_rb, n_lh, n_chunk, per = wide // ROWS, ny // LANES, wide // CHUNK, planes // GROUPS
    ty_hi, ty_lo = split_table(gauss_table(ny))
    kx_hi, kx_lo = split_table(np.kron(np.eye(planes), gauss_table(wide)))
    side = planes * wide
    any_ = pl.BlockSpec(memory_space=pl.ANY)

    def columns(lead, depth):
        return pltpu.VMEM((*lead, depth, ROWS, LANES), F32)

    def field(depth):
        return pltpu.VMEM((nf, depth, wide, ny), F32)

    scratch = [
        columns((n_rb, n_lh), planes + 2 * BOUND),
        columns((n_rb, n_lh), planes + 2 * BOUND + 2 * RADIUS),
        field(planes + 2 * RADIUS),
        pltpu.VMEM((n_chunk, GROUPS, nf, 2, coils, per, CHUNK, ny), BF16),
        pltpu.VMEM((n_chunk, GROUPS, 2, coils, per, CHUNK, ny), BF16),
        field(planes + 2 * RADIUS),
        pltpu.VMEM((planes, wide, ny), F32),
        columns((n_rb, n_lh), planes + 2 * BOUND),
        columns((n_chunk, n_lh), planes + 2 * BOUND),
        columns((n_chunk, 5), planes),
        field(planes + 2 * RADIUS),
        pltpu.VMEM((side, ny), BF16),
        pltpu.VMEM((side, ny), BF16),
        field(planes),
        pltpu.VMEM((ny, ny), BF16),
        pltpu.VMEM((ny, ny), BF16),
        pltpu.VMEM((side, side), BF16),
        pltpu.VMEM((side, side), BF16),
        pltpu.SemaphoreType.DMA((48,)),
        pltpu.SemaphoreType.DMA((64,)),
        pltpu.SemaphoreType.DMA((64,)),
    ]
    return pl.pallas_call(
        functools.partial(kernel, (n_slab, nf * n_frame, coils)),
        out_shape=(
            jax.ShapeDtypeStruct((planes, wide, ny), F32),
            jax.ShapeDtypeStruct((nf, planes, wide, ny), F32),
        ),
        in_specs=[any_] * 8,
        out_specs=(any_, any_),
        scratch_shapes=scratch,
        compiler_params=pltpu.CompilerParams(
            collective_id=0, has_side_effects=True, vmem_limit_bytes=50 * 1024 * 1024
        ),
        cost_estimate=pl.CostEstimate(flops=10**8, bytes_accessed=2 * 10**7, transcendentals=0),
    )(*[pltpu.with_memory_space_constraint(x, pltpu.HBM) for x in (
        template, displacement, coil_images, sensitivities,
        jnp.asarray(ty_hi), jnp.asarray(ty_lo), jnp.asarray(kx_hi), jnp.asarray(kx_lo))])


def solution(mesh):
    placed = (
        P("slab", None, None),
        P("frame", "slab", None, None),
        P("frame", None, None, "slab", None, None),
        P(None, None, "slab", None, None),
    )
    return jax.shard_map(
        per_device,
        mesh=mesh,
        in_specs=placed,
        out_specs=(P("slab", None, None), P("frame", "slab", None, None)),
        check_vma=False,
    )
```

```python
import functools

import jax
import jax.numpy as jnp
import numpy as np
from jax import lax
from jax.experimental import pallas as pl
from jax.experimental.pallas import tpu as pltpu
from jax.sharding import PartitionSpec as P

BOUND = 8
RADIUS = 4
ROWS = 8
LANES = 128
CHUNK = 16
GROUPS = 4
MESH = pl.DeviceIdType.MESH
F32 = jnp.float32
BF16 = jnp.bfloat16


def gauss_weights():
    j = np.arange(-RADIUS, RADIUS + 1, dtype=np.float64)
    spread = RADIUS * 0.5
    w = np.exp(-j * j / (2.0 * spread * spread))
    return w / w.sum()


def gauss_table(length):
    w = gauss_weights()
    table = np.zeros((length, length), np.float64)
    for j in range(-RADIUS, RADIUS + 1):
        table += w[j + RADIUS] * np.eye(length, k=j)
    return table


def split_table(table):
    hi = table.astype(np.float32).astype(BF16)
    lo = (table - hi.astype(np.float64)).astype(np.float32).astype(BF16)
    return hi, lo


def locate(d):
    m3 = d >= 0.0
    r = jnp.where(m3, d, d + 8.0)
    m2 = r >= 4.0
    r = jnp.where(m2, r - 4.0, r)
    m1 = r >= 2.0
    r = jnp.where(m1, r - 2.0, r)
    m0 = r >= 1.0
    t = jnp.where(m0, r - 1.0, r)
    return m3, m2, m1, m0, t


def gather_line(place, plane):
    m3, m2, m1, m0, t = place
    a = [plane(j) for j in range(17)]
    b = [jnp.where(m3, a[j + 8], a[j]) for j in range(9)]
    c = [jnp.where(m2, b[j + 4], b[j]) for j in range(5)]
    e = [jnp.where(m1, c[j + 2], c[j]) for j in range(3)]
    lo = jnp.where(m0, e[1], e[0])
    hi = jnp.where(m0, e[2], e[1])
    return lo + t * (hi - lo)


def scatter_line(place, value):
    m3, m2, m1, m0, t = place
    hi = t * value
    lo = value - hi
    zero = jnp.zeros_like(value)
    e = [jnp.where(m0, zero, lo), jnp.where(m0, lo, hi), jnp.where(m0, hi, zero)]

    def spread(src, mask, step):
        n = len(src)
        out = []
        for j in range(n + step):
            low = src[j] if j < n else zero
            high = src[j - step] if j >= step else zero
            out.append(jnp.where(mask, high, low))
        return out

    return spread(spread(spread(e, m1, 2), m2, 4), m3, 8)


def kernel(cfg, tmpl, disp, coil, sens, ty_hi_h, ty_lo_h, kx_hi_h, kx_lo_h, out_t, out_d,
           tx, rx, dv, cb, sb, comb, ener, adj, radj, ra, mv,
           slope, bottom, shi, slo, obuf, ty_hi, ty_lo, kx_hi, kx_lo, lsem, ssem, rsem):
    n_slab, frames_all, coils = cfg
    nf, planes, wide, ny = obuf.shape
    n_rb = wide // ROWS
    n_lh = ny // LANES
    n_chunk = wide // CHUNK
    per = planes // GROUPS
    reach = BOUND + RADIUS
    f = lax.axis_index("frame")
    s = lax.axis_index("slab")
    h = lax.rem(f, 2)
    q = lax.div(f, 2)
    o = 1 - q
    mate = f + 1 - 2 * h
    across = f + 2 - 4 * q
    at_slab = {k: lax.rem(s + k + n_slab, n_slab) for k in (-2, -1, 0, 1, 2)}
    exists = {-2: s > 1, -1: s > 0, 0: None, 1: s < n_slab - 1, 2: s < n_slab - 2}

    counter = [0]

    def local(src, dst):
        copy = pltpu.make_async_copy(src, dst, lsem.at[counter[0]])
        counter[0] += 1
        copy.start()
        return copy

    load_t = [local(tmpl.at[:, pl.ds(ROWS * b, ROWS), pl.ds(LANES * l, LANES)], tx.at[b, l, pl.ds(BOUND, planes)])
              for b in range(n_rb) for l in range(n_lh)]
    def clear(ref, *index):
        ref[index] = jnp.zeros_like(ref[index])

    every = slice(None)

    @pl.when(s == 0)
    def _():
        clear(tx, every, every, slice(0, BOUND))
        clear(rx, every, every, slice(0, reach))
        clear(dv, every, slice(0, RADIUS))
        clear(comb, every, slice(0, RADIUS))

    @pl.when(s == 1)
    def _():
        clear(rx, every, every, slice(0, RADIUS))

    @pl.when(s == n_slab - 2)
    def _():
        clear(rx, every, every, slice(planes + reach + BOUND, None))

    @pl.when(s == n_slab - 1)
    def _():
        clear(tx, every, every, slice(BOUND + planes, None))
        clear(rx, every, every, slice(planes + reach, None))
        clear(dv, every, slice(planes + RADIUS, None))
        clear(comb, every, slice(planes + RADIUS, None))

    barrier = pltpu.get_barrier_semaphore()
    near = ((mate, s), (across, s), (f, at_slab[1]), (f, at_slab[-1]))
    for dev in near:
        pl.semaphore_signal(barrier, inc=1, device_id=dev, device_id_type=MESH)
    load_d = local(disp, dv.at[:, pl.ds(RADIUS, planes)])
    load_c = {}
    for c in range(n_chunk):
        for g in range(GROUPS):
            zs, xs = pl.ds(per * g, per), pl.ds(CHUNK * c, CHUNK)
            load_c[c, g] = (
                local(sens.at[:, :, zs, xs, :], sb.at[c, g]),
                local(coil.at[:, :, :, zs, xs, :], cb.at[c, g]),
            )
    load_k = [local(a, b) for a, b in ((ty_hi_h, ty_hi), (ty_lo_h, ty_lo), (kx_hi_h, kx_hi), (kx_lo_h, kx_lo))]

    pl.semaphore_wait(barrier, len(near))

    rcount = [0]
    pending = []

    def maybe(condition, action):
        if condition is None:
            action()
        else:
            pl.when(condition)(action)

    class Remote:
        def __init__(self, src, dst, frame, step=0):
            n = rcount[0]
            rcount[0] += 1
            self.copy = pltpu.make_async_remote_copy(
                src_ref=src, dst_ref=dst, send_sem=ssem.at[n], recv_sem=rsem.at[n],
                device_id=(frame, at_slab[step]), device_id_type=MESH)
            self.send_if, self.recv_if = exists[step], exists[-step]
            maybe(self.send_if, lambda: self.copy.start())
            pending.append(self)

        def recv(self):
            maybe(self.recv_if, lambda: self.copy.wait_recv())

        def sent(self):
            maybe(self.send_if, lambda: self.copy.wait_send())

    own = pl.ds(BOUND, planes)
    low = pl.ds(0, BOUND)
    high = pl.ds(BOUND + planes, BOUND)
    inner = pl.ds(reach, planes)
    wire = {}

    def arrive(*keys):
        for key in keys:
            for item in wire[key]:
                item.recv()

    def template_out(c):
        rb = 2 * c + h
        wire["t", c] = [Remote(tx.at[rb, :, own], tx.at[rb, :, low], f, 1),
                        Remote(tx.at[rb, :, own], tx.at[rb, :, high], f, -1)]

    def template_pass(c):
        rb = 2 * c + h
        arrive(("t", c))
        wire["tf", c] = [Remote(tx.at[rb, :, part], tx.at[rb, :, part], mate) for part in (low, high)]

    def template_in(c):
        arrive(("tf", c))

    def disp_out():
        wire["d"] = [
            Remote(dv.at[:, pl.ds(planes, RADIUS)], dv.at[:, pl.ds(0, RADIUS)], f, 1),
            Remote(dv.at[:, pl.ds(RADIUS, RADIUS)], dv.at[:, pl.ds(planes + RADIUS, RADIUS)], f, -1)]

    def comb_out(i_f):
        part = comb.at[i_f]
        wire["c", i_f] = [
            Remote(part.at[pl.ds(planes, RADIUS)], part.at[pl.ds(0, RADIUS)], f, 1),
            Remote(part.at[pl.ds(RADIUS, RADIUS)], part.at[pl.ds(planes + RADIUS, RADIUS)], f, -1)]

    def combine(c, g):
        for copy in load_c[c, g]:
            copy.wait()

        def step(zz, _):
            acc = None
            for p in range(2):
                for k in range(coils):
                    w = sb[c, g, p, k, zz].astype(F32)
                    vals = [cb[c, g, i, p, k, zz].astype(F32) * w for i in range(nf)] + [w * w]
                    acc = vals if acc is None else [x + v for x, v in zip(acc, vals)]
            z = per * g + zz
            xs = pl.ds(CHUNK * c, CHUNK)
            for i in range(nf):
                comb[i, RADIUS + z, xs, :] = acc[i]
            ener[z, xs, :] = acc[nf]
            return 0

        lax.fori_loop(0, per, step, 0)

    def adjoint(c):
        def step(i, _):
            l = lax.rem(i, n_lh)
            rb = 2 * c + lax.div(i, n_lh)
            lanes = pl.ds(pl.multiple_of(l * LANES, LANES), LANES)
            rows = pl.ds(pl.multiple_of(rb * ROWS, ROWS), ROWS)
            sums = [None] * (planes + 2 * BOUND)
            for z in range(planes):
                en = ener[z, rows, lanes]
                for i_f in range(nf):
                    place = locate(dv[i_f, RADIUS + z, rows, lanes])
                    warped = gather_line(place, lambda j: tx[rb, l, z + j])
                    value = comb[i_f, RADIUS + z, rows, lanes] - en * warped
                    for j, term in enumerate(scatter_line(place, value)):
                        sums[z + j] = term if sums[z + j] is None else sums[z + j] + term
            for at, total in enumerate(sums):
                adj[rb, l, at] = total
            return 0

        lax.fori_loop(0, 2 * n_lh, step, 0)

    def adj_mate(c):
        wire["am", c] = [Remote(adj.at[2 * c + 1 - h], radj.at[c], mate)]

    def adj_out(c):
        rb = 2 * c + h
        arrive(("am", c))
        for part in (high, low):
            adj[rb, o, part] = adj[rb, o, part] + radj[c, o, part]
        sends = [Remote(adj.at[rb, o, high], ra.at[c, 0], across, 1),
                 Remote(adj.at[rb, o, low], ra.at[c, 1], across, -1)]
        for part in (high, low):
            adj[rb, q, part] = adj[rb, q, part] + radj[c, q, part]
        sends += [Remote(adj.at[rb, q, high], ra.at[c, 2], f, 1),
                  Remote(adj.at[rb, q, low], ra.at[c, 3], f, -1)]
        adj[rb, o, own] = adj[rb, o, own] + radj[c, o, own]
        sends += [Remote(adj.at[rb, o, own], ra.at[c, 4], across)]
        adj[rb, q, own] = adj[rb, q, own] + radj[c, q, own]
        wire["a", c] = sends

    def refresh(c):
        rb = 2 * c + h
        arrive(("a", c))

        total = adj[rb, q, own] + ra[c, 4]
        for up, sides in ((True, (0, 2)), (False, (1, 3))):
            for k in sides:
                ok = exists[-1] if up else exists[1]
                total = total + jnp.where(ok, ra[c, k], 0.0)
        rx[rb, q, inner] = tx[rb, q, own] + total * (1.0 / frames_all)
        mine = rx.at[rb, q]
        whole = mine.at[inner]
        sends = []
        for frame in (across, f):
            sends += [Remote(whole, mine.at[pl.ds(RADIUS, BOUND)], frame, 1),
                      Remote(whole, mine.at[pl.ds(planes + reach, BOUND)], frame, -1)]
        sends += [Remote(whole, whole, across)]
        wire["r", c] = sends

    def far_out(c):
        mine = rx.at[2 * c + h, q]
        tail, head = mine.at[pl.ds(reach + RADIUS, RADIUS)], mine.at[pl.ds(reach, RADIUS)]
        wire["far", c] = []
        for frame in (across, f):
            wire["far", c] += [Remote(tail, mine.at[pl.ds(0, RADIUS)], frame, 2),
                               Remote(head, mine.at[pl.ds(planes + reach + BOUND, RADIUS)], frame, -2)]

    def refresh_pass(c):
        rb = 2 * c + h
        arrive(("r", c))
        near = rx.at[rb, :, pl.ds(RADIUS, planes + 2 * BOUND)]
        wire["rf", c] = [Remote(near, near, mate)]

    def refresh_in(c):
        arrive(("rf", c))

    def far_pass(c):
        rb = 2 * c + h
        arrive(("far", c))
        ends = [rx.at[rb, :, pl.ds(0, RADIUS)], rx.at[rb, :, pl.ds(planes + reach + BOUND, RADIUS)]]
        wire["ff", c] = [Remote(end, end, mate) for end in ends]

    def far_in(c):
        arrive(("ff", c))

    saves = []

    def save_template(b):
        for l in range(n_lh):
            saves.append(local(rx.at[b, l, inner], out_t.at[:, pl.ds(ROWS * b, ROWS), pl.ds(LANES * l, LANES)]))

    OWN, HALO = (RADIUS, RADIUS), (0, planes + RADIUS)

    def warp(c, group):
        first, apart = group

        def step(i, _):
            col = lax.div(i, 2)
            base = first + apart * lax.rem(i, 2)
            l = lax.rem(col, n_lh)
            rb = 2 * c + lax.div(col, n_lh)
            lanes = pl.ds(pl.multiple_of(l * LANES, LANES), LANES)
            rows = pl.ds(pl.multiple_of(rb * ROWS, ROWS), ROWS)
            for k in range(RADIUS):
                p = base + k
                for i_f in range(nf):
                    mv[i_f, p, rows, lanes] = gather_line(locate(dv[i_f, p, rows, lanes]), lambda j: rx[rb, l, p + j])
            return 0

        lax.fori_loop(0, 4 * n_lh, step, 0)

    def push(b, group):
        row = lax.broadcasted_iota(jnp.int32, (ROWS, LANES), 0)
        lane = lax.broadcasted_iota(jnp.int32, (ROWS, LANES), 1)
        first, last = row == 0, row == ROWS - 1
        left, right = lane == 0, lane == LANES - 1
        rows = pl.ds(b * ROWS, ROWS)
        zero = jnp.zeros((ROWS, LANES), F32)

        def step(i, _):
            for k in range(RADIUS):
                p = group[0] + i * group[1] + k
                at = p + BOUND
                for l in range(n_lh):
                    lanes = pl.ds(l * LANES, LANES)
                    here = rx[b, l, at]
                    before = pltpu.roll(rx[b - 1, l, at], 1, 0) if b > 0 else zero
                    after = pltpu.roll(rx[b + 1, l, at], ROWS - 1, 0) if b < n_rb - 1 else zero
                    prev_x = jnp.where(first, before, pltpu.roll(here, 1, 0))
                    next_x = jnp.where(last, after, pltpu.roll(here, ROWS - 1, 0))
                    before = pltpu.roll(rx[b, l - 1, at], 1, 1) if l > 0 else zero
                    after = pltpu.roll(rx[b, l + 1, at], LANES - 1, 1) if l < n_lh - 1 else zero
                    prev_y = jnp.where(left, before, pltpu.roll(here, 1, 1))
                    next_y = jnp.where(right, after, pltpu.roll(here, LANES - 1, 1))
                    gx = (next_x - prev_x) * 0.5
                    gy = (next_y - prev_y) * 0.5
                    gz = (rx[b, l, at + 1] - rx[b, l, at - 1]) * 0.5
                    floor = gx * gx + gy * gy + gz * gz + 1.0
                    if group is HALO:
                        slope[i, l, k, rows] = gz
                        bottom[i, l, k, rows] = floor
                        continue
                    for i_f in range(nf):
                        miss = comb[i_f, p, rows, lanes] - mv[i_f, p, rows, lanes]
                        mv[i_f, p, rows, lanes] = dv[i_f, p, rows, lanes] + miss * gz / (floor + miss * miss)
            return 0

        lax.fori_loop(0, 2, step, 0)

    def push_halo(i_f):
        def step(i, _):
            side = lax.div(i, n_lh)
            l = lax.rem(i, n_lh)
            lanes = pl.ds(pl.multiple_of(l * LANES, LANES), LANES)
            for k in range(RADIUS):
                p = side * (planes + RADIUS) + k
                gz = slope[side, l, k]
                miss = comb[i_f, p, :, lanes] - mv[i_f, p, :, lanes]
                mv[i_f, p, :, lanes] = dv[i_f, p, :, lanes] + miss * gz / (bottom[side, l, k] + miss * miss)
            return 0

        lax.fori_loop(0, 2 * n_lh, step, 0)

        @pl.when(s == 0)
        def _():
            clear(mv, i_f, slice(0, RADIUS))

        @pl.when(s == n_slab - 1)
        def _():
            clear(mv, i_f, slice(planes + RADIUS, None))

    weights = [float(w) for w in gauss_weights()]

    def halves(value):
        hi = value.astype(BF16)
        return hi, (value - hi.astype(F32)).astype(BF16)

    def dot3(a_hi, a_lo, b_hi, b_lo):
        dot = functools.partial(jnp.dot, preferred_element_type=F32)
        return dot(a_hi, b_hi) + (dot(a_lo, b_hi) + dot(a_hi, b_lo))

    def taps(i_f, z, inside):
        total = obuf[i_f, z] if not inside else None
        for j in range(2 * RADIUS + 1):
            if inside == (RADIUS <= z + j < planes + RADIUS):
                term = weights[j] * mv[i_f, z + j]
                total = term if total is None else total + term
        return total

    def smooth_own(i_f):
        for z in range(planes):
            obuf[i_f, z] = taps(i_f, z, True)

    def smooth(i_f):
        for z in range(planes):
            hi, lo = halves(taps(i_f, z, False))
            at = pl.ds(z * wide, wide)
            shi[at, :] = hi
            slo[at, :] = lo
        along_y = dot3(shi[...], slo[...], ty_hi[...], ty_lo[...])
        y_hi, y_lo = halves(along_y)
        done = dot3(kx_hi[...], kx_lo[...], y_hi, y_lo)
        obuf[i_f] = (BOUND * jnp.tanh(done * (1.0 / BOUND))).reshape(planes, wide, ny)
        saves.append(local(obuf.at[i_f], out_d.at[i_f]))

    for copy in load_t:
        copy.wait()
    for c in range(n_chunk):
        template_out(c)
    for g in range(GROUPS):
        combine(0, g)
    load_d.wait()
    disp_out()
    combine(1, 0)
    combine(1, 1)
    template_pass(0)
    combine(1, 2)
    combine(1, 3)
    template_pass(1)
    template_in(0)
    adjoint(0)
    adj_mate(0)
    template_in(1)
    adjoint(1)
    adj_mate(1)
    adj_out(0)
    adj_out(1)
    refresh(0)
    refresh(1)
    far_out(0)
    far_out(1)
    comb_out(0)
    comb_out(1)
    for copy in load_k:
        copy.wait()
    refresh_pass(0)
    refresh_pass(1)
    refresh_in(0)
    warp(0, OWN)
    push(0, OWN)
    save_template(0)
    save_template(1)
    refresh_in(1)
    warp(1, OWN)
    save_template(2)
    save_template(3)
    far_pass(0)
    for b in range(1, n_rb):
        push(b, OWN)
    far_pass(1)
    for i_f in range(nf):
        smooth_own(i_f)
    arrive("d")
    far_in(0)
    warp(0, HALO)
    far_in(1)
    warp(1, HALO)
    for b in range(n_rb):
        push(b, HALO)
    for i_f in range(nf):
        arrive(("c", i_f))
        push_halo(i_f)
        smooth(i_f)
    for item in pending:
        item.sent()
    for copy in saves:
        copy.wait()


def per_device(template, displacement, coil_images, sensitivities):
    nf, planes, wide, ny = displacement.shape
    coils = coil_images.shape[2]
    n_slab = lax.axis_size("slab")
    n_frame = lax.axis_size("frame")
    n_rb, n_lh, n_chunk, per = wide // ROWS, ny // LANES, wide // CHUNK, planes // GROUPS
    ty_hi, ty_lo = split_table(gauss_table(ny))
    kx_hi, kx_lo = split_table(np.kron(np.eye(planes), gauss_table(wide)))
    side = planes * wide
    any_ = pl.BlockSpec(memory_space=pl.ANY)

    def columns(lead, depth):
        return pltpu.VMEM((*lead, depth, ROWS, LANES), F32)

    def field(depth):
        return pltpu.VMEM((nf, depth, wide, ny), F32)

    scratch = [
        columns((n_rb, n_lh), planes + 2 * BOUND),
        columns((n_rb, n_lh), planes + 2 * BOUND + 2 * RADIUS),
        field(planes + 2 * RADIUS),
        pltpu.VMEM((n_chunk, GROUPS, nf, 2, coils, per, CHUNK, ny), BF16),
        pltpu.VMEM((n_chunk, GROUPS, 2, coils, per, CHUNK, ny), BF16),
        field(planes + 2 * RADIUS),
        pltpu.VMEM((planes, wide, ny), F32),
        columns((n_rb, n_lh), planes + 2 * BOUND),
        columns((n_chunk, n_lh), planes + 2 * BOUND),
        columns((n_chunk, 5), planes),
        field(planes + 2 * RADIUS),
        pltpu.VMEM((2, n_lh, RADIUS, wide, LANES), F32),
        pltpu.VMEM((2, n_lh, RADIUS, wide, LANES), F32),
        pltpu.VMEM((side, ny), BF16),
        pltpu.VMEM((side, ny), BF16),
        field(planes),
        pltpu.VMEM((ny, ny), BF16),
        pltpu.VMEM((ny, ny), BF16),
        pltpu.VMEM((side, side), BF16),
        pltpu.VMEM((side, side), BF16),
        pltpu.SemaphoreType.DMA((48,)),
        pltpu.SemaphoreType.DMA((64,)),
        pltpu.SemaphoreType.DMA((64,)),
    ]
    return pl.pallas_call(
        functools.partial(kernel, (n_slab, nf * n_frame, coils)),
        out_shape=(
            jax.ShapeDtypeStruct((planes, wide, ny), F32),
            jax.ShapeDtypeStruct((nf, planes, wide, ny), F32),
        ),
        in_specs=[any_] * 8,
        out_specs=(any_, any_),
        scratch_shapes=scratch,
        compiler_params=pltpu.CompilerParams(
            collective_id=0, has_side_effects=True, vmem_limit_bytes=50 * 1024 * 1024
        ),
        cost_estimate=pl.CostEstimate(flops=10**8, bytes_accessed=2 * 10**7, transcendentals=0),
    )(*[pltpu.with_memory_space_constraint(x, pltpu.HBM) for x in (
        template, displacement, coil_images, sensitivities,
        jnp.asarray(ty_hi), jnp.asarray(ty_lo), jnp.asarray(kx_hi), jnp.asarray(kx_lo))])


def solution(mesh):
    placed = (
        P("slab", None, None),
        P("frame", "slab", None, None),
        P("frame", None, None, "slab", None, None),
        P(None, None, "slab", None, None),
    )
    return jax.shard_map(
        per_device,
        mesh=mesh,
        in_specs=placed,
        out_specs=(P("slab", None, None), P("frame", "slab", None, None)),
        check_vma=False,
    )
```

```python
import functools

import jax
import jax.numpy as jnp
import numpy as np
from jax import lax
from jax.experimental import pallas as pl
from jax.experimental.pallas import tpu as pltpu
from jax.sharding import PartitionSpec as P

BOUND = 8
RADIUS = 4
ROWS = 8
LANES = 128
CHUNK = 16
GROUPS = 4
MESH = pl.DeviceIdType.MESH
F32 = jnp.float32
BF16 = jnp.bfloat16


def gauss_weights():
    j = np.arange(-RADIUS, RADIUS + 1, dtype=np.float64)
    spread = RADIUS * 0.5
    w = np.exp(-j * j / (2.0 * spread * spread))
    return w / w.sum()


def gauss_table(length):
    w = gauss_weights()
    table = np.zeros((length, length), np.float64)
    for j in range(-RADIUS, RADIUS + 1):
        table += w[j + RADIUS] * np.eye(length, k=j)
    return table


def split_table(table):
    hi = table.astype(np.float32).astype(BF16)
    lo = (table - hi.astype(np.float64)).astype(np.float32).astype(BF16)
    return hi, lo


def locate(d):
    m3 = d >= 0.0
    r = jnp.where(m3, d, d + 8.0)
    m2 = r >= 4.0
    r = jnp.where(m2, r - 4.0, r)
    m1 = r >= 2.0
    r = jnp.where(m1, r - 2.0, r)
    m0 = r >= 1.0
    t = jnp.where(m0, r - 1.0, r)
    return m3, m2, m1, m0, t


def gather_line(place, plane):
    m3, m2, m1, m0, t = place
    a = [plane(j) for j in range(17)]
    b = [jnp.where(m3, a[j + 8], a[j]) for j in range(9)]
    c = [jnp.where(m2, b[j + 4], b[j]) for j in range(5)]
    e = [jnp.where(m1, c[j + 2], c[j]) for j in range(3)]
    lo = jnp.where(m0, e[1], e[0])
    hi = jnp.where(m0, e[2], e[1])
    return lo + t * (hi - lo)


def scatter_line(place, value):
    m3, m2, m1, m0, t = place
    hi = t * value
    lo = value - hi
    zero = jnp.zeros_like(value)
    e = [jnp.where(m0, zero, lo), jnp.where(m0, lo, hi), jnp.where(m0, hi, zero)]

    def spread(src, mask, step):
        n = len(src)
        out = []
        for j in range(n + step):
            low = src[j] if j < n else zero
            high = src[j - step] if j >= step else zero
            out.append(jnp.where(mask, high, low))
        return out

    return spread(spread(spread(e, m1, 2), m2, 4), m3, 8)


def kernel(cfg, tmpl, disp, coil, sens, ty_hi_h, ty_lo_h, kx_hi_h, kx_lo_h, out_t, out_d,
           tx, rx, dv, cb, sb, comb, ener, adj, radj, ra, mv,
           slope, bottom, shi, slo, obuf, ty_hi, ty_lo, kx_hi, kx_lo, lsem, ssem, rsem):
    n_slab, frames_all, coils = cfg
    nf, planes, wide, ny = obuf.shape
    n_rb = wide // ROWS
    n_lh = ny // LANES
    n_chunk = wide // CHUNK
    per = planes // GROUPS
    reach = BOUND + RADIUS
    f = lax.axis_index("frame")
    s = lax.axis_index("slab")
    h = lax.rem(f, 2)
    q = lax.div(f, 2)
    o = 1 - q
    mate = f + 1 - 2 * h
    across = f + 2 - 4 * q
    at_slab = {k: lax.rem(s + k + n_slab, n_slab) for k in (-2, -1, 0, 1, 2)}
    exists = {-2: s > 1, -1: s > 0, 0: None, 1: s < n_slab - 1, 2: s < n_slab - 2}

    counter = [0]

    def local(src, dst):
        copy = pltpu.make_async_copy(src, dst, lsem.at[counter[0]])
        counter[0] += 1
        copy.start()
        return copy

    load_t = [local(tmpl.at[:, pl.ds(ROWS * b, ROWS), pl.ds(LANES * l, LANES)], tx.at[b, l, pl.ds(BOUND, planes)])
              for b in range(n_rb) for l in range(n_lh)]
    def clear(ref, *index):
        ref[index] = jnp.zeros_like(ref[index])

    every = slice(None)

    @pl.when(s == 0)
    def _():
        clear(tx, every, every, slice(0, BOUND))
        clear(rx, every, every, slice(0, reach))
        clear(dv, every, slice(0, RADIUS))
        clear(comb, every, slice(0, RADIUS))

    @pl.when(s == 1)
    def _():
        clear(rx, every, every, slice(0, RADIUS))

    @pl.when(s == n_slab - 2)
    def _():
        clear(rx, every, every, slice(planes + reach + BOUND, None))

    @pl.when(s == n_slab - 1)
    def _():
        clear(tx, every, every, slice(BOUND + planes, None))
        clear(rx, every, every, slice(planes + reach, None))
        clear(dv, every, slice(planes + RADIUS, None))
        clear(comb, every, slice(planes + RADIUS, None))

    barrier = pltpu.get_barrier_semaphore()
    near = ((mate, s), (across, s), (f, at_slab[1]), (f, at_slab[-1]))
    for dev in near:
        pl.semaphore_signal(barrier, inc=1, device_id=dev, device_id_type=MESH)
    load_d = local(disp, dv.at[:, pl.ds(RADIUS, planes)])
    load_c = {}
    for c in range(n_chunk):
        for g in range(GROUPS):
            zs, xs = pl.ds(per * g, per), pl.ds(CHUNK * c, CHUNK)
            load_c[c, g] = (
                local(sens.at[:, :, zs, xs, :], sb.at[c, g]),
                local(coil.at[:, :, :, zs, xs, :], cb.at[c, g]),
            )
    load_k = [local(a, b) for a, b in ((ty_hi_h, ty_hi), (ty_lo_h, ty_lo), (kx_hi_h, kx_hi), (kx_lo_h, kx_lo))]

    pl.semaphore_wait(barrier, len(near))

    rcount = [0]
    pending = []

    def maybe(condition, action):
        if condition is None:
            action()
        else:
            pl.when(condition)(action)

    class Remote:
        def __init__(self, src, dst, frame, step=0):
            n = rcount[0]
            rcount[0] += 1
            self.copy = pltpu.make_async_remote_copy(
                src_ref=src, dst_ref=dst, send_sem=ssem.at[n], recv_sem=rsem.at[n],
                device_id=(frame, at_slab[step]), device_id_type=MESH)
            self.send_if, self.recv_if = exists[step], exists[-step]
            maybe(self.send_if, lambda: self.copy.start())
            pending.append(self)

        def recv(self):
            maybe(self.recv_if, lambda: self.copy.wait_recv())

        def sent(self):
            maybe(self.send_if, lambda: self.copy.wait_send())

    own = pl.ds(BOUND, planes)
    low = pl.ds(0, BOUND)
    high = pl.ds(BOUND + planes, BOUND)
    inner = pl.ds(reach, planes)
    wire = {}

    def arrive(*keys):
        for key in keys:
            for item in wire[key]:
                item.recv()

    def template_out(c):
        rb = 2 * c + h
        wire["t", c] = [Remote(tx.at[rb, :, own], tx.at[rb, :, low], f, 1),
                        Remote(tx.at[rb, :, own], tx.at[rb, :, high], f, -1)]

    def template_pass(c):
        rb = 2 * c + h
        arrive(("t", c))
        wire["tf", c] = [Remote(tx.at[rb, :, part], tx.at[rb, :, part], mate) for part in (low, high)]

    def template_in(c):
        arrive(("tf", c))

    def disp_out():
        wire["d"] = [
            Remote(dv.at[:, pl.ds(planes, RADIUS)], dv.at[:, pl.ds(0, RADIUS)], f, 1),
            Remote(dv.at[:, pl.ds(RADIUS, RADIUS)], dv.at[:, pl.ds(planes + RADIUS, RADIUS)], f, -1)]

    def comb_out(i_f):
        part = comb.at[i_f]
        wire["c", i_f] = [
            Remote(part.at[pl.ds(planes, RADIUS)], part.at[pl.ds(0, RADIUS)], f, 1),
            Remote(part.at[pl.ds(RADIUS, RADIUS)], part.at[pl.ds(planes + RADIUS, RADIUS)], f, -1)]

    def combine(c, g):
        for copy in load_c[c, g]:
            copy.wait()

        def step(zz, _):
            acc = None
            for p in range(2):
                for k in range(coils):
                    w = sb[c, g, p, k, zz].astype(F32)
                    vals = [cb[c, g, i, p, k, zz].astype(F32) * w for i in range(nf)] + [w * w]
                    acc = vals if acc is None else [x + v for x, v in zip(acc, vals)]
            z = per * g + zz
            xs = pl.ds(CHUNK * c, CHUNK)
            for i in range(nf):
                comb[i, RADIUS + z, xs, :] = acc[i]
            ener[z, xs, :] = acc[nf]
            return 0

        lax.fori_loop(0, per, step, 0)

    def adjoint(rb):
        def step(l, _):
            lanes = pl.ds(pl.multiple_of(l * LANES, LANES), LANES)
            rows = pl.ds(pl.multiple_of(rb * ROWS, ROWS), ROWS)
            sums = [None] * (planes + 2 * BOUND)
            for z in range(planes):
                en = ener[z, rows, lanes]
                for i_f in range(nf):
                    place = locate(dv[i_f, RADIUS + z, rows, lanes])
                    warped = gather_line(place, lambda j: tx[rb, l, z + j])
                    value = comb[i_f, RADIUS + z, rows, lanes] - en * warped
                    for j, term in enumerate(scatter_line(place, value)):
                        sums[z + j] = term if sums[z + j] is None else sums[z + j] + term
            for at, total in enumerate(sums):
                adj[rb, l, at] = total
            return 0

        lax.fori_loop(0, n_lh, step, 0)

    def adj_mate(c):
        wire["am", c] = [Remote(adj.at[2 * c + 1 - h], radj.at[c], mate)]

    def adj_out(c):
        rb = 2 * c + h
        arrive(("am", c))
        for part in (high, low):
            adj[rb, o, part] = adj[rb, o, part] + radj[c, o, part]
        sends = [Remote(adj.at[rb, o, high], ra.at[c, 0], across, 1),
                 Remote(adj.at[rb, o, low], ra.at[c, 1], across, -1)]
        for part in (high, low):
            adj[rb, q, part] = adj[rb, q, part] + radj[c, q, part]
        sends += [Remote(adj.at[rb, q, high], ra.at[c, 2], f, 1),
                  Remote(adj.at[rb, q, low], ra.at[c, 3], f, -1)]
        adj[rb, o, own] = adj[rb, o, own] + radj[c, o, own]
        sends += [Remote(adj.at[rb, o, own], ra.at[c, 4], across)]
        adj[rb, q, own] = adj[rb, q, own] + radj[c, q, own]
        wire["a", c] = sends

    def refresh(c):
        rb = 2 * c + h
        arrive(("a", c))

        total = adj[rb, q, own] + ra[c, 4]
        for up, sides in ((True, (0, 2)), (False, (1, 3))):
            for k in sides:
                ok = exists[-1] if up else exists[1]
                total = total + jnp.where(ok, ra[c, k], 0.0)
        rx[rb, q, inner] = tx[rb, q, own] + total * (1.0 / frames_all)
        mine = rx.at[rb, q]
        whole = mine.at[inner]
        sends = []
        for frame in (across, f):
            sends += [Remote(whole, mine.at[pl.ds(RADIUS, BOUND)], frame, 1),
                      Remote(whole, mine.at[pl.ds(planes + reach, BOUND)], frame, -1)]
        sends += [Remote(whole, whole, across)]
        wire["r", c] = sends

    def far_out(c):
        mine = rx.at[2 * c + h, q]
        tail, head = mine.at[pl.ds(reach + RADIUS, RADIUS)], mine.at[pl.ds(reach, RADIUS)]
        wire["far", c] = []
        for frame in (across, f):
            wire["far", c] += [Remote(tail, mine.at[pl.ds(0, RADIUS)], frame, 2),
                               Remote(head, mine.at[pl.ds(planes + reach + BOUND, RADIUS)], frame, -2)]

    def refresh_pass(c):
        rb = 2 * c + h
        arrive(("r", c))
        near = rx.at[rb, :, pl.ds(RADIUS, planes + 2 * BOUND)]
        wire["rf", c] = [Remote(near, near, mate)]

    def refresh_in(c):
        arrive(("rf", c))

    def far_pass(c):
        rb = 2 * c + h
        arrive(("far", c))
        ends = [rx.at[rb, :, pl.ds(0, RADIUS)], rx.at[rb, :, pl.ds(planes + reach + BOUND, RADIUS)]]
        wire["ff", c] = [Remote(end, end, mate) for end in ends]

    def far_in(c):
        arrive(("ff", c))

    saves = []

    def save_template(b):
        for l in range(n_lh):
            saves.append(local(rx.at[b, l, inner], out_t.at[:, pl.ds(ROWS * b, ROWS), pl.ds(LANES * l, LANES)]))

    OWN, HALO = (RADIUS, RADIUS), (0, planes + RADIUS)

    def warp(c, group):
        first, apart = group

        def step(i, _):
            col = lax.div(i, 2)
            base = first + apart * lax.rem(i, 2)
            l = lax.rem(col, n_lh)
            rb = 2 * c + lax.div(col, n_lh)
            lanes = pl.ds(pl.multiple_of(l * LANES, LANES), LANES)
            rows = pl.ds(pl.multiple_of(rb * ROWS, ROWS), ROWS)
            for k in range(RADIUS):
                p = base + k
                for i_f in range(nf):
                    mv[i_f, p, rows, lanes] = gather_line(locate(dv[i_f, p, rows, lanes]), lambda j: rx[rb, l, p + j])
            return 0

        lax.fori_loop(0, 4 * n_lh, step, 0)

    def push(b, group):
        row = lax.broadcasted_iota(jnp.int32, (ROWS, LANES), 0)
        lane = lax.broadcasted_iota(jnp.int32, (ROWS, LANES), 1)
        first, last = row == 0, row == ROWS - 1
        left, right = lane == 0, lane == LANES - 1
        rows = pl.ds(b * ROWS, ROWS)
        zero = jnp.zeros((ROWS, LANES), F32)

        def step(i, _):
            for k in range(RADIUS):
                p = group[0] + i * group[1] + k
                at = p + BOUND
                for l in range(n_lh):
                    lanes = pl.ds(l * LANES, LANES)
                    here = rx[b, l, at]
                    before = pltpu.roll(rx[b - 1, l, at], 1, 0) if b > 0 else zero
                    after = pltpu.roll(rx[b + 1, l, at], ROWS - 1, 0) if b < n_rb - 1 else zero
                    prev_x = jnp.where(first, before, pltpu.roll(here, 1, 0))
                    next_x = jnp.where(last, after, pltpu.roll(here, ROWS - 1, 0))
                    before = pltpu.roll(rx[b, l - 1, at], 1, 1) if l > 0 else zero
                    after = pltpu.roll(rx[b, l + 1, at], LANES - 1, 1) if l < n_lh - 1 else zero
                    prev_y = jnp.where(left, before, pltpu.roll(here, 1, 1))
                    next_y = jnp.where(right, after, pltpu.roll(here, LANES - 1, 1))
                    gx = (next_x - prev_x) * 0.5
                    gy = (next_y - prev_y) * 0.5
                    gz = (rx[b, l, at + 1] - rx[b, l, at - 1]) * 0.5
                    floor = gx * gx + gy * gy + gz * gz + 1.0
                    if group is HALO:
                        slope[i, l, k, rows] = gz
                        bottom[i, l, k, rows] = floor
                        continue
                    for i_f in range(nf):
                        miss = comb[i_f, p, rows, lanes] - mv[i_f, p, rows, lanes]
                        mv[i_f, p, rows, lanes] = dv[i_f, p, rows, lanes] + miss * gz / (floor + miss * miss)
            return 0

        lax.fori_loop(0, 2, step, 0)

    def push_halo(i_f):
        def step(i, _):
            side = lax.div(i, n_lh)
            l = lax.rem(i, n_lh)
            lanes = pl.ds(pl.multiple_of(l * LANES, LANES), LANES)
            for k in range(RADIUS):
                p = side * (planes + RADIUS) + k
                gz = slope[side, l, k]
                miss = comb[i_f, p, :, lanes] - mv[i_f, p, :, lanes]
                mv[i_f, p, :, lanes] = dv[i_f, p, :, lanes] + miss * gz / (bottom[side, l, k] + miss * miss)
            return 0

        lax.fori_loop(0, 2 * n_lh, step, 0)

        @pl.when(s == 0)
        def _():
            clear(mv, i_f, slice(0, RADIUS))

        @pl.when(s == n_slab - 1)
        def _():
            clear(mv, i_f, slice(planes + RADIUS, None))

    weights = [float(w) for w in gauss_weights()]

    def halves(value):
        hi = value.astype(BF16)
        return hi, (value - hi.astype(F32)).astype(BF16)

    def dot3(a_hi, a_lo, b_hi, b_lo):
        dot = functools.partial(jnp.dot, preferred_element_type=F32)
        return dot(a_hi, b_hi) + (dot(a_lo, b_hi) + dot(a_hi, b_lo))

    def taps(i_f, z, inside):
        total = obuf[i_f, z] if not inside else None
        for j in range(2 * RADIUS + 1):
            if inside == (RADIUS <= z + j < planes + RADIUS):
                term = weights[j] * mv[i_f, z + j]
                total = term if total is None else total + term
        return total

    def smooth_own(i_f):
        for z in range(planes):
            obuf[i_f, z] = taps(i_f, z, True)

    def smooth(i_f):
        for z in range(planes):
            hi, lo = halves(taps(i_f, z, False))
            at = pl.ds(z * wide, wide)
            shi[at, :] = hi
            slo[at, :] = lo
        along_y = dot3(shi[...], slo[...], ty_hi[...], ty_lo[...])
        y_hi, y_lo = halves(along_y)
        done = dot3(kx_hi[...], kx_lo[...], y_hi, y_lo)
        obuf[i_f] = (BOUND * jnp.tanh(done * (1.0 / BOUND))).reshape(planes, wide, ny)
        saves.append(local(obuf.at[i_f], out_d.at[i_f]))

    for copy in load_t:
        copy.wait()
    for c in range(n_chunk):
        template_out(c)
    for g in range(GROUPS):
        combine(0, g)
    load_d.wait()
    disp_out()
    combine(1, 0)
    combine(1, 1)
    template_pass(0)
    combine(1, 2)
    combine(1, 3)
    template_pass(1)
    for c in range(n_chunk):
        adjoint(2 * c + h)
    for c in range(n_chunk):
        template_in(c)
        adjoint(2 * c + 1 - h)
        adj_mate(c)
    adj_out(0)
    adj_out(1)
    refresh(0)
    far_out(0)
    refresh(1)
    far_out(1)
    comb_out(0)
    comb_out(1)
    for copy in load_k:
        copy.wait()
    refresh_pass(0)
    refresh_pass(1)
    refresh_in(0)
    warp(0, OWN)
    push(0, OWN)
    save_template(0)
    save_template(1)
    refresh_in(1)
    warp(1, OWN)
    save_template(2)
    save_template(3)
    far_pass(0)
    for b in range(1, n_rb):
        push(b, OWN)
    far_pass(1)
    for i_f in range(nf):
        smooth_own(i_f)
    arrive("d")
    far_in(0)
    warp(0, HALO)
    far_in(1)
    warp(1, HALO)
    for b in range(n_rb):
        push(b, HALO)
    for i_f in range(nf):
        arrive(("c", i_f))
        push_halo(i_f)
        smooth(i_f)
    for item in pending:
        item.sent()
    for copy in saves:
        copy.wait()


def hand_out(t_in, d_in, t_out, d_out, sem):
    copies = [pltpu.make_async_copy(d_in, d_out, sem.at[0]), pltpu.make_async_copy(t_in, t_out, sem.at[1])]
    for copy in copies:
        copy.start()
    for copy in copies:
        copy.wait()


def per_device(template, displacement, coil_images, sensitivities):
    nf, planes, wide, ny = displacement.shape
    coils = coil_images.shape[2]
    n_slab = lax.axis_size("slab")
    n_frame = lax.axis_size("frame")
    n_rb, n_lh, n_chunk, per = wide // ROWS, ny // LANES, wide // CHUNK, planes // GROUPS
    ty_hi, ty_lo = split_table(gauss_table(ny))
    kx_hi, kx_lo = split_table(np.kron(np.eye(planes), gauss_table(wide)))
    side = planes * wide
    any_ = pl.BlockSpec(memory_space=pl.ANY)

    def columns(lead, depth):
        return pltpu.VMEM((*lead, depth, ROWS, LANES), F32)

    def field(depth):
        return pltpu.VMEM((nf, depth, wide, ny), F32)

    scratch = [
        columns((n_rb, n_lh), planes + 2 * BOUND),
        columns((n_rb, n_lh), planes + 2 * BOUND + 2 * RADIUS),
        field(planes + 2 * RADIUS),
        pltpu.VMEM((n_chunk, GROUPS, nf, 2, coils, per, CHUNK, ny), BF16),
        pltpu.VMEM((n_chunk, GROUPS, 2, coils, per, CHUNK, ny), BF16),
        field(planes + 2 * RADIUS),
        pltpu.VMEM((planes, wide, ny), F32),
        columns((n_rb, n_lh), planes + 2 * BOUND),
        columns((n_chunk, n_lh), planes + 2 * BOUND),
        columns((n_chunk, 5), planes),
        field(planes + 2 * RADIUS),
        pltpu.VMEM((2, n_lh, RADIUS, wide, LANES), F32),
        pltpu.VMEM((2, n_lh, RADIUS, wide, LANES), F32),
        pltpu.VMEM((side, ny), BF16),
        pltpu.VMEM((side, ny), BF16),
        field(planes),
        pltpu.VMEM((ny, ny), BF16),
        pltpu.VMEM((ny, ny), BF16),
        pltpu.VMEM((side, side), BF16),
        pltpu.VMEM((side, side), BF16),
        pltpu.SemaphoreType.DMA((48,)),
        pltpu.SemaphoreType.DMA((64,)),
        pltpu.SemaphoreType.DMA((64,)),
    ]
    results = pl.pallas_call(
        functools.partial(kernel, (n_slab, nf * n_frame, coils)),
        out_shape=(
            jax.ShapeDtypeStruct((planes, wide, ny), F32),
            jax.ShapeDtypeStruct((nf, planes, wide, ny), F32),
        ),
        in_specs=[any_] * 8,
        out_specs=(any_, any_),
        scratch_shapes=scratch,
        compiler_params=pltpu.CompilerParams(
            collective_id=0, has_side_effects=True, vmem_limit_bytes=50 * 1024 * 1024
        ),
        cost_estimate=pl.CostEstimate(flops=10**8, bytes_accessed=2 * 10**7, transcendentals=0),
    )(*[pltpu.with_memory_space_constraint(x, pltpu.HBM) for x in (
        template, displacement, coil_images, sensitivities,
        jnp.asarray(ty_hi), jnp.asarray(ty_lo), jnp.asarray(kx_hi), jnp.asarray(kx_lo))])
    return pl.pallas_call(
        hand_out,
        out_shape=tuple(jax.ShapeDtypeStruct(x.shape, F32) for x in results),
        in_specs=[pl.BlockSpec(memory_space=pltpu.VMEM)] * 2,
        out_specs=(any_, any_),
        scratch_shapes=[pltpu.SemaphoreType.DMA((2,))],
        cost_estimate=pl.CostEstimate(flops=0, bytes_accessed=16 * planes * wide * ny, transcendentals=0),
    )(*[pltpu.with_memory_space_constraint(x, pltpu.VMEM) for x in results])


def solution(mesh):
    placed = (
        P("slab", None, None),
        P("frame", "slab", None, None),
        P("frame", None, None, "slab", None, None),
        P(None, None, "slab", None, None),
    )
    return jax.shard_map(
        per_device,
        mesh=mesh,
        in_specs=placed,
        out_specs=(P("slab", None, None), P("frame", "slab", None, None)),
        check_vma=False,
    )
```
